256 devices in a mesh: seq: 8 (over y, core), tensor: 8 (over z), adapter: 4 (over x).
Axes of the slice: x: 4, y: 4, z: 8, core: 2. Of those that a mesh axis runs over, the one named last changes fastest.
Arguments:
- tokens: bfloat16 [4, 8192, 4096], P('adapter', 'seq', 'tensor'), may hold values from -6 to 6
- in_weight: bfloat16 [4096, 3, 2048], P(None, None, 'tensor'), may hold values from -0.09375 to 0.09375
- adapter_down_maps: bfloat16 [32, 4096, 64], P(('seq', 'adapter'), 'tensor'), may hold values from -0.09375 to 0.09375
- adapter_up_maps: bfloat16 [32, 64, 3, 2048], P(('seq', 'adapter'), None, None, 'tensor'), may hold values from -0.359375 to 0.359375
- short_filter: float32 [7, 3, 2048], P(None, None, 'tensor'), may hold values from -2.4 to 2.4
- long_filter: float32 [128, 2048], P(None, 'tensor'), may hold values from -0.53033006 to 0.53033006
- skip: float32 [2048], P('tensor'), may hold values from -1 to 1
- out_weight: bfloat16 [2048, 4096], P('tensor'), may hold values from -0.1875 to 0.1875
- adapter_ids: int32 [4, 8192, 1], P('adapter', 'seq'), may hold values from 0 to 31; in each aligned block of 1024 rows (0 to 1023, 1024 to 2047, ..., all dimensions but the last counted through in order) at most 96 rows name the same one
Outputs:
- mixed: bfloat16 [4, 8192, 4096], P('adapter', 'seq', 'tensor')
The draws below stay inside these ranges and needn't reach their ends.
Inputs may be any that keep to these rules, and one draw needn't show every extreme that they name: `adapter_ids`: among the rows of one device, no adapter set is named by more than 96 rows.
All inputs are finite; a program needn't handle non-finite values.
Results may differ from the reference program's by a relative error of at most 0.0082.
Values may be sent and summed in bfloat16 or wider, within the bound.
No kernel may reach another device: no remote copies, remote signals or barrier semaphores. Data moves between devices by JAX's collectives and lax.ppermute only.
A program may use at most 128 MiB of HBM per device.

```python
import math
import jax
import jax.numpy as jnp
import numpy as np
from jax import lax

D = 4096
DM = 2048
RANK = 64
STAPS = 7
LTAPS = 128
TOK_DEV = 1024
ADAPTERS = 32
CAP = 96
BATCH = 4
LENGTH = 8192


def strengthened(result, rng, source, target, blocks, factor):
    owner, partner = [(jnp.arange(result.shape[dim]) // (result.shape[dim] // blocks)).reshape([-1 if axis == dim else 1 for axis in range(result.ndim)]) for dim in (source, target)]
    chosen = jax.random.permutation(rng, blocks)[partner]
    strong = (owner == chosen) | (owner == (partner + blocks // 2) % blocks)
    return jnp.where(strong, factor * result, result)


def steps_of(key, dims, shards, smallest, largest):
    factor_of, own = 1.0, jax.random.fold_in(key, 6)
    for dim, shards_of in shards:
        draws = jnp.exp(jax.random.uniform(jax.random.fold_in(own, dim), (shards_of,), jnp.float32, smallest / len(shards), largest / len(shards)))
        factor_of = factor_of * jnp.repeat(draws, dims[dim] // shards_of).reshape([-1 if axis == dim else 1 for axis in range(len(dims))])
    return factor_of


def assign_block(key, own, number, rows, amount, top, most, skew):
    order = jax.random.permutation(key, amount)
    heavy_load, ordinary = shares(amount, rows * top, most, skew, True), shares(amount, rows * top, most, skew, False)
    places = jnp.arange(amount)

    def named(lengths, offset_by):
        used = int((lengths > 0).sum())
        fixed = max(1, used // 4)
        shifted = fixed + (places - fixed + offset_by * (used - fixed)) % max(1, amount - fixed)
        return jnp.zeros((amount,), jnp.int32).at[order[jnp.where(places < fixed, places, shifted)]].set(jnp.asarray(lengths, jnp.int32))

    lengths = jnp.where(number % 4 == 0, named(heavy_load, number // 4), named(ordinary, number - number // 4 - 1))
    mixed = jax.random.permutation(jax.random.fold_in(own, 3), amount)
    giver, sink = mixed[0:amount // 2 * 2:2], mixed[1:amount // 2 * 2:2]
    margin = jnp.minimum(lengths[giver] - 1, most - lengths[sink]) // 2
    margin = jnp.where((giver == order[0]) | (sink == order[0]) | (lengths[sink] == 0), 0, jnp.maximum(margin, 0))
    shifted = jax.random.randint(jax.random.fold_in(own, 4), (amount // 2,), 0, 1 << 20) % (margin + 1)
    lengths = lengths.at[giver].add(-shifted).at[sink].add(shifted)
    items = jnp.searchsorted(jnp.cumsum(lengths), jnp.arange(rows * top), side="right").astype(jnp.int32)
    table = items.reshape(top, rows).T
    table = table[jax.random.permutation(jax.random.fold_in(own, 1), rows)]
    offset_by = jax.random.randint(jax.random.fold_in(own, 2), (rows, 1), 0, top)
    return jnp.take_along_axis(table, (jnp.arange(top)[None, :] + offset_by) % top, axis=1)


def shares(amount, total, limit, skew, full):
    weights = [(1 << 20) // math.isqrt(standing ** skew) + 1 for standing in range(1, amount + 1)]
    largest = limit if full else min(limit, max(-(-total // amount), total * weights[0] // sum(weights)))
    least = 1 if total - largest >= amount - 1 else 0
    counts, surplus = [largest] + [least] * (amount - 1), total - largest - least * (amount - 1)
    while surplus > 0:
        candidates = [i for i in range(1, amount) if counts[i] < largest] or [i for i in range(1, amount) if counts[i] < limit]
        mass, remaining = sum([weights[i] for i in candidates]), surplus
        for i in candidates:
            more = min(limit - counts[i], max(1, remaining * weights[i] // mass), surplus)
            counts[i] = counts[i] + more
            surplus = surplus - more
    return np.array(counts)


def bell_draw(rng, shape, deviation, most, cuts=(), kind=jnp.bfloat16):
    array = jax.random.normal(rng, shape, jnp.float32) * deviation
    if len(cuts) > 0:
        array = steps_of(rng, shape, cuts, -0.22, 0.18) * array
    return jnp.clip(array, min=-most, max=most).astype(kind)


def bell_draw_with(rng, shape, spread, limit, shards, heavy, dtype=jnp.bfloat16):
    entries = spread * jax.random.normal(rng, shape, jnp.float32)
    if shards:
        entries = entries * steps_of(rng, shape, shards, -0.22, 0.18)
    return jnp.clip(strengthened(entries, jax.random.fold_in(rng, 3), *heavy), -limit, limit).astype(dtype)


def setup_inputs(seed: int = 0) -> dict:
    splits = jax.random.split(jax.random.key(seed), 10)
    tokens = bell_draw(splits[0], (BATCH, LENGTH, D), 1.0, 6.0, ((0, 4), (1, 8), (2, 8)))
    in_weight = bell_draw(splits[1], (D, 3, DM), D ** -0.5, 0.09375, ((2, 8),))
    adapter_down_maps = bell_draw(splits[2], (ADAPTERS, D, RANK), D ** -0.5, 0.09375, ((0, 32), (1, 8)))
    adapter_up_maps = bell_draw(splits[3], (ADAPTERS, RANK, 3, DM), 0.06, 0.359375, ((0, 32), (3, 8)))
    short_filter = bell_draw(splits[4], (STAPS, 3, DM), 0.4, 2.4, ((2, 8),), jnp.float32)
    long_filter = bell_draw(splits[5], (LTAPS, DM), (LTAPS ** -0.5), 0.53033006, ((1, 8),), jnp.float32)
    skip = jnp.clip(jax.random.uniform(splits[6], (DM,), jnp.float32, -1.0, 1.0) * steps_of(splits[6], (DM,), ((0, 8),), -0.4, 0.0), -1.0, 1.0)
    out_weight = bell_draw_with(splits[7], (DM, D), DM ** -0.5, 0.1875, ((0, 8),), (0, 1, 8, 2.0))
    adapter_ids_keys = jax.random.split(jax.random.fold_in(splits[8], 1), BATCH * LENGTH // TOK_DEV)
    adapter_ids_turns = jax.random.permutation(jax.random.fold_in(splits[8], 3), BATCH * LENGTH // TOK_DEV)
    adapter_ids = jax.vmap(lambda own, number: assign_block(jax.random.fold_in(splits[8], 2), own, number, TOK_DEV, ADAPTERS, 1, CAP, 2))(adapter_ids_keys, adapter_ids_turns).reshape((BATCH, LENGTH, 1))
    return dict(tokens=tokens, in_weight=in_weight, adapter_down_maps=adapter_down_maps, adapter_up_maps=adapter_up_maps, short_filter=short_filter, long_filter=long_filter, skip=skip, out_weight=out_weight, adapter_ids=adapter_ids)


def low_rank_block(block_arguments, adapter_down_maps, adapter_up_maps):
    block_rows, block_owner = block_arguments
    down_rows = adapter_down_maps[block_owner].astype(jnp.float32)
    low_codes = jnp.einsum('td,tdr->tr', block_rows.astype(jnp.float32), down_rows, precision=lax.Precision.HIGHEST)
    low_codes = low_codes.astype(jnp.bfloat16)
    up_rows = adapter_up_maps[block_owner].reshape(block_owner.shape[0], RANK, 3 * DM).astype(jnp.float32)
    grown = jnp.einsum('tr,trm->tm', low_codes.astype(jnp.float32), up_rows, precision=lax.Precision.HIGHEST)
    return grown.astype(jnp.bfloat16)


def reference(tokens, in_weight, adapter_down_maps, adapter_up_maps, short_filter, long_filter, skip, out_weight, adapter_ids):
    flat_rows = tokens.reshape(BATCH * LENGTH, D)
    flat_owner = adapter_ids.reshape(BATCH * LENGTH).astype(jnp.int32)
    projected = jnp.dot(flat_rows, in_weight.reshape(D, 3 * DM), preferred_element_type=jnp.float32)
    adapter_correction = lax.map(lambda adapter_pair: low_rank_block(adapter_pair, adapter_down_maps, adapter_up_maps),
                            (flat_rows.reshape(-1, 32, D), flat_owner.reshape(-1, 32)))
    adapter_correction = adapter_correction.reshape(BATCH * LENGTH, 3 * DM)
    mixed_in = (projected + adapter_correction.astype(jnp.float32)).astype(jnp.bfloat16)
    mixed_in = mixed_in.reshape(BATCH, LENGTH, 3 * DM).astype(jnp.float32)
    short_taps = short_filter.reshape(STAPS, 3 * DM)
    padded = jnp.pad(mixed_in, ((0, 0), (STAPS - 1, 0), (0, 0)))
    filtered = jnp.zeros((BATCH, LENGTH, 3 * DM), jnp.float32)
    for tap in range(STAPS):
        filtered = filtered + short_taps[tap] * padded[:, STAPS - 1 - tap:STAPS - 1 - tap + LENGTH]
    query_gate = filtered[:, :, :DM]
    key_value = (filtered[:, :, DM:2 * DM] * filtered[:, :, 2 * DM:]).astype(jnp.bfloat16)
    key_float = key_value.astype(jnp.float32)
    long_pad = jnp.pad(key_float, ((0, 0), (LTAPS - 1, 0), (0, 0)))

    def add_tap(tap, running):
        begin = (LTAPS - 1 - tap).astype(jnp.int32)
        window = lax.dynamic_slice_in_dim(long_pad, begin, LENGTH, 1)
        weights = lax.dynamic_slice_in_dim(long_filter, tap.astype(jnp.int32), 1, 0)
        return running + weights[0] * window

    long_out = lax.fori_loop(0, LTAPS, add_tap, jnp.zeros((BATCH, LENGTH, DM), jnp.float32))
    long_out = long_out + skip * key_float
    gated = (query_gate * long_out).astype(jnp.bfloat16)
    mixed = jnp.dot(gated.reshape(BATCH * LENGTH, DM), out_weight, preferred_element_type=jnp.float32)
    return mixed.astype(jnp.bfloat16).reshape(BATCH, LENGTH, D)
```

```python
import jax
import jax.numpy as jnp
from jax import lax
from jax.experimental import pallas as pl
from jax.experimental.pallas import tpu as pltpu
from jax.sharding import PartitionSpec as P

F32 = jnp.float32
BF16 = jnp.bfloat16
PARAMS = pltpu.CompilerParams(vmem_limit_bytes=40 * 1024 * 1024)


def moved(block, axis, distance):
    n = lax.axis_size(axis)
    return lax.ppermute(block, axis, [(i, (i + distance) % n) for i in range(n)])


def nt_dot(a, b):
    return lax.dot_general(a, b, (((1,), (1,)), ((), ())), preferred_element_type=F32)


def codes_kernel(tok_ref, slot_ref, near_ref, far_ref, out_ref):
    tok = tok_ref[...]
    slot = slot_ref[...]
    total = jnp.zeros((64, tok.shape[0]), F32)
    for side, ref in enumerate((near_ref, far_ref)):
        products = nt_dot(ref[...], tok)
        for own in range(16):
            total = total + jnp.where(
                slot == side * 16 + own, products[own * 64 : own * 64 + 64], 0.0
            )
    for j in range(out_ref.shape[0]):
        out_ref[j] = total[:, 128 * j : 128 * j + 128]


def partial_codes(tok, slot, near, far):
    rows, depth = tok.shape
    block = 256
    return pl.pallas_call(
        codes_kernel,
        grid=(rows // block,),
        in_specs=[
            pl.BlockSpec((block, depth), lambda i: (i, 0)),
            pl.BlockSpec((1, block), lambda i: (0, i)),
            pl.BlockSpec(near.shape, lambda i: (0, 0)),
            pl.BlockSpec(far.shape, lambda i: (0, 0)),
        ],
        out_specs=pl.BlockSpec((block // 128, 64, 128), lambda i: (i, 0, 0)),
        out_shape=jax.ShapeDtypeStruct((rows // 128, 64, 128), F32),
        compiler_params=PARAMS,
    )(tok, slot, near, far)


def weight_spec(weight, k):
    parts, depth, channels = weight.shape
    return pl.BlockSpec(
        (parts, depth // 8, channels), lambda i, place: (0, (place[0] + 8 - k) % 8, 0)
    )


def tag_spec():
    return pl.BlockSpec((16, 128), lambda i, place: (0, 0))


def projecting(place, acc, pieces, ks, weight, tied=(), after=()):
    rows, depth = pieces[0][0].shape[0], pieces[0][0].shape[1]
    rows = max(piece.shape[0] - first * 256 for piece, first in pieces[1:])
    block = 256
    parts, _, channels = weight.shape
    width = parts * channels
    old = [] if acc is None else [acc]
    n, m = len(pieces), len(tied)

    def kernel(place_ref, *refs):
        total_in, refs = refs[: len(old)], refs[len(old) :]
        tokens, weights = refs[:n], refs[n : 2 * n]
        tags_in = refs[2 * n : 2 * n + m]
        outs = refs[2 * n + m + len(after) :]
        loaded = [piece[...] for piece in tokens]
        for c in range(parts):
            lanes = slice(c * channels, (c + 1) * channels)
            total = jnp.dot(loaded[0], weights[0][c], preferred_element_type=F32)
            for piece, ref in zip(loaded[1:], weights[1:]):
                total = total + jnp.dot(piece, ref[c], preferred_element_type=F32)
            if old:
                total = total + total_in[0][:, lanes]
            outs[0][:, lanes] = total
        for source, target in zip(tags_in, outs[1:]):
            target[...] = source[...]

    def piece_spec(first):
        return pl.BlockSpec((block, depth), lambda i, place: (i + first, 0))

    acc_spec = pl.BlockSpec((block, width), lambda i, place: (i, 0))
    return pl.pallas_call(
        kernel,
        grid_spec=pltpu.PrefetchScalarGridSpec(
            num_scalar_prefetch=1,
            grid=(rows // block,),
            in_specs=[acc_spec for _ in old]
            + [piece_spec(first) for _, first in pieces]
            + [weight_spec(weight, k) for k in ks]
            + [tag_spec() for _ in tied]
            + [pl.BlockSpec(memory_space=pl.ANY) for _ in after],
            out_specs=[acc_spec] + [tag_spec() for _ in tied],
        ),
        out_shape=[jax.ShapeDtypeStruct((rows, width), F32)]
        + [jax.ShapeDtypeStruct((16, 128), BF16) for _ in tied],
        compiler_params=PARAMS,
    )(place, *old, *[piece for piece, _ in pieces], *[weight for _ in ks], *tied, *after)


def tie(block, tag):
    return lax.dynamic_update_slice(block, tag, (0, 0))


def mixing(place, acc, thirds, fourths, weight, codes, ids, gathered, taps, first_block, rims):
    rows, width = acc.shape
    block = 256
    steps = rows // block
    depth = thirds[0].shape[1]
    channels = width // 3
    split = fourths[0].shape[0] // block

    def kernel(place_ref, acc_ref, f3_ref, b3_ref, *refs):
        opposite_refs, refs = refs[: len(fourths)], refs[len(fourths) :]
        w3_ref, w5_ref, w4_ref, codes_ref, ids_ref, u0_ref, u1_ref, u2_ref, taps_ref = refs[:9]
        outs = refs[9:]
        mixed_ref = outs[0]
        step = pl.program_id(0)
        opposite = opposite_refs[0][...]
        if len(fourths) > 1:
            opposite = jnp.where(step < split, opposite, opposite_refs[1][...])
        packed = codes_ref[...].astype(F32)
        low = jnp.concatenate([packed[j].T for j in range(2)], axis=0).astype(BF16)
        low = jnp.concatenate([low, low], axis=1)
        upper = lax.broadcasted_iota(jnp.int32, (1, 128), 1) // 64
        ids_block = ids_ref[...]
        zero = jnp.zeros_like(low)
        spread = jnp.concatenate(
            [jnp.where(ids_block == upper + 2 * pair, low, zero) for pair in range(16)], axis=1
        )
        for c, ref in enumerate((u0_ref, u1_ref, u2_ref)):
            lanes = slice(c * channels, (c + 1) * channels)
            total = acc_ref[:, lanes]
            total = total + jnp.dot(f3_ref[...], w3_ref[c], preferred_element_type=F32)
            total = total + jnp.dot(b3_ref[...], w5_ref[c], preferred_element_type=F32)
            total = total + jnp.dot(opposite, w4_ref[c], preferred_element_type=F32)
            up = ref[...].reshape(-1, channels)
            delta = jnp.dot(spread, up, preferred_element_type=F32).astype(BF16)
            mixed_ref[:, lanes] = (total + delta.astype(F32)).astype(BF16)

        for slot, at in enumerate(rims):

            @pl.when(step == at)
            def _():
                rim_ref = outs[1]
                branches = []
                for c in (1, 2):
                    lanes = slice(c * channels, (c + 1) * channels)
                    tail = mixed_ref[:, lanes].astype(F32)
                    running = jnp.zeros((128, channels), F32)
                    for tap in range(7):
                        running = (
                            running
                            + taps_ref[c, tap : tap + 1, :] * tail[block - 128 - tap : block - tap]
                        )
                    branches.append(running)
                rim_ref[slot, :128] = (branches[0] * branches[1]).astype(BF16)
                for c in range(3):
                    rim_ref[slot, 128 + 16 * c : 144 + 16 * c] = mixed_ref[
                        block - 16 :, c * channels : (c + 1) * channels
                    ]

    def up_spec(c):
        return pl.BlockSpec((32, 64, channels), lambda i, place: (0, c, 0))

    def rows_spec(array, start=0):
        last = array.shape[0] // block - 1
        return pl.BlockSpec(
            (block, depth), lambda i, place: (jnp.clip(i - start, 0, last), 0)
        )

    out_specs = [pl.BlockSpec((block, width), lambda i, place: (i, 0))]
    out_shape = [jax.ShapeDtypeStruct((rows, width), BF16)]
    if rims:
        out_specs.append(pl.BlockSpec((len(rims), 176, channels), lambda i, place: (0, 0, 0)))
        out_shape.append(jax.ShapeDtypeStruct((len(rims), 176, channels), BF16))
    return pl.pallas_call(
        kernel,
        grid_spec=pltpu.PrefetchScalarGridSpec(
            num_scalar_prefetch=1,
            grid=(steps,),
            in_specs=[
                pl.BlockSpec((block, width), lambda i, place: (i, 0)),
                rows_spec(thirds[0]),
                rows_spec(thirds[1]),
            ]
            + [rows_spec(array, split * j) for j, array in enumerate(fourths)]
            + [
                weight_spec(weight, 3),
                weight_spec(weight, 5),
                weight_spec(weight, 4),
                pl.BlockSpec((2, 64, 128), lambda i, place: (i + first_block, 0, 0)),
                pl.BlockSpec((block, 1), lambda i, place: (i + first_block, 0)),
                up_spec(0),
                up_spec(1),
                up_spec(2),
                pl.BlockSpec(taps.shape, lambda i, place: (0, 0, 0)),
            ],
            out_specs=out_specs,
        ),
        out_shape=out_shape,
        compiler_params=PARAMS,
    )(
        place, acc, *thirds, *fourths, weight, weight, weight, codes, ids,
        gathered, gathered, gathered, taps,
    )


def filtering(parts, rim, taps, long_filter, skip):
    block = 128
    width = parts[0][0].shape[1]
    channels = width // 3
    steps = sum(count for _, _, count in parts)

    def kernel(*refs):
        mixed_refs, refs = refs[: len(parts)], refs[len(parts) :]
        rim_ref, taps_ref, long_ref, skip_ref, gated_ref, before_ref, window_ref = refs
        step = pl.program_id(0)
        mixed = mixed_refs[0][...]
        if len(parts) > 1:
            mixed = jnp.where(step < parts[0][2], mixed, mixed_refs[1][...])
        mixed = mixed.astype(F32)

        @pl.when(step == 0)
        def _():
            window_ref[:128] = rim_ref[:128].astype(F32)
            for c in range(3):
                before_ref[:, c * channels : (c + 1) * channels] = rim_ref[
                    128 + 16 * c : 144 + 16 * c
                ].astype(F32)

        @pl.when(step > 0)
        def _():
            window_ref[:128] = window_ref[block : block + 128]

        filtered = []
        for c in range(3):
            lanes = slice(c * channels, (c + 1) * channels)
            extended = jnp.concatenate([before_ref[:, lanes], mixed[:, lanes]], axis=0)
            running = jnp.zeros((block, channels), F32)
            for tap in range(7):
                running = running + taps_ref[c, tap : tap + 1, :] * extended[16 - tap : 16 - tap + block]
            filtered.append(running)
        before_ref[...] = mixed[block - 16 :]
        key_value = (filtered[1] * filtered[2]).astype(BF16)
        window_ref[128:] = key_value.astype(F32)
        for lane in range(channels // 128):
            lanes = slice(lane * 128, lane * 128 + 128)
            out = skip_ref[:, lanes] * window_ref[128 : 128 + block, lanes]
            for r in range(8):
                partial = jnp.zeros((block + 8, 128), F32)
                for q in range(16):
                    tap = 8 * q + r
                    start = 120 - 8 * q
                    partial = (
                        partial
                        + long_ref[tap : tap + 1, lanes]
                        * window_ref[start : start + block + 8, lanes]
                    )
                out = out + partial[8 - r : 8 - r + block]
            gated_ref[:, lanes] = (filtered[0][:, lanes] * out).astype(BF16)

    def part_spec(before, first, count):
        return pl.BlockSpec(
            (block, width), lambda i: (jnp.clip(i - before, 0, count - 1) + first, 0)
        )

    in_specs, before = [], 0
    for _, first, count in parts:
        in_specs.append(part_spec(before, first, count))
        before += count
    whole = lambda a: pl.BlockSpec(a.shape, lambda i: (0,) * a.ndim)
    return pl.pallas_call(
        kernel,
        grid=(steps,),
        in_specs=in_specs + [whole(a) for a in (rim, taps, long_filter, skip)],
        out_specs=pl.BlockSpec((block, channels), lambda i: (i, 0)),
        out_shape=jax.ShapeDtypeStruct((steps * block, channels), BF16),
        scratch_shapes=[
            pltpu.VMEM((16, width), F32),
            pltpu.VMEM((128 + block, channels), F32),
        ],
        compiler_params=PARAMS,
    )(*[part for part, _, _ in parts], rim, taps, long_filter, skip)


def out_kernel(*refs):
    pieces, (low_ref, high_ref), out_ref = refs[:9], refs[9:11], refs[-1]
    step = pl.program_id(0)
    channels = low_ref.shape[2]
    opposite = jnp.where(step == 0, pieces[7][...], pieces[8][...])
    blocks = [piece[...] for piece in pieces[:7]] + [opposite]
    for side, ref in enumerate((low_ref, high_ref)):
        total = jnp.zeros((out_ref.shape[0], channels), F32)
        for k, block in zip((0, 1, 7, 2, 6, 3, 5, 4), blocks):
            weight = ref[4 * k : 4 * k + 4].reshape(-1, channels)
            total = total + jnp.dot(block, weight, preferred_element_type=F32)
        out_ref[:, side * channels : (side + 1) * channels] = total.astype(BF16)


def out_projection(pieces, gathered, previous, first_block, rows_all):
    rows, channels = pieces[0].shape
    block = rows // 2
    operands = list(pieces) + [gathered, gathered]
    in_specs = (
        [pl.BlockSpec((block, channels), lambda i: (i, 0))] * 7
        + [pl.BlockSpec((block, channels), lambda i: (0, 0))] * 2
        + [
            pl.BlockSpec((32, 64, channels), lambda i: (0, 3, 0)),
            pl.BlockSpec((32, 64, channels), lambda i: (0, 4, 0)),
        ]
    )
    aliases = {}
    if previous is not None:
        aliases = {len(operands): 0}
        operands.append(previous)
        in_specs.append(pl.BlockSpec(memory_space=pl.ANY))
    return pl.pallas_call(
        out_kernel,
        grid=(2,),
        in_specs=in_specs,
        out_specs=pl.BlockSpec((block, 2 * channels), lambda i: (i + first_block, 0)),
        out_shape=jax.ShapeDtypeStruct((rows_all, 2 * channels), BF16),
        input_output_aliases=aliases,
        compiler_params=PARAMS,
    )(*operands)


def both_ways(ahead, back):
    return moved(ahead, "tensor", 1), moved(back, "tensor", -1)


def ring(block):
    half = block.shape[0] // 2
    ahead = back = block
    pieces = [block]
    for _ in range(3):
        ahead, back = both_ways(ahead, back)
        pieces += [ahead, back]
    return pieces + list(both_ways(ahead[:half], back[half:]))


def per_device(
    tokens,
    in_weight,
    adapter_down_maps,
    adapter_up_maps,
    short_filter,
    long_filter,
    skip,
    out_weight,
    adapter_ids,
):
    tok = tokens[0]
    ids = adapter_ids[0]
    rows, depth = tok.shape
    channels = in_weight.shape[2]
    seq, tensor, adapter = (lax.axis_index(name) for name in ("seq", "tensor", "adapter"))
    place = tensor.astype(jnp.int32).reshape(1)
    weight = in_weight.transpose(1, 0, 2)
    taps = short_filter.transpose(1, 0, 2)
    skip_row = skip.reshape(1, -1)

    quarter = out_weight.shape[0] // 4
    out_rows = lax.dynamic_slice(
        out_weight,
        (adapter * quarter, ((tensor + seq) % 8) * depth),
        (quarter, depth),
    )
    out_rows = lax.ppermute(
        out_rows,
        ("seq", "tensor"),
        [(s * 8 + z, s * 8 + (z + s) % 8) for s in range(8) for z in range(8)],
    )
    parcel = jnp.concatenate(
        [
            adapter_up_maps[0].transpose(1, 0, 2).reshape(-1, channels),
            out_rows[:, :channels],
            out_rows[:, channels:],
        ],
        0,
    )
    gathered = lax.all_gather(parcel, ("seq", "adapter"), axis=0)

    down = adapter_down_maps[0].T
    down = jnp.concatenate(
        [down, moved(down, "adapter", 1), moved(down, "adapter", 2), moved(down, "adapter", -1)], 0
    )
    down = jnp.concatenate(
        [down, moved(down, "seq", 2), moved(down, "seq", 4), moved(down, "seq", -2)], 0
    )
    far = lax.ppermute(down, "seq", [(i, i ^ 1) for i in range(8)])
    named_seq, named_adapter = ids // 4, ids % 4
    slot = (
        (((seq % 2) ^ (named_seq % 2)) * 4 + (seq // 2 + 4 - named_seq // 2) % 4) * 4
        + (adapter + 4 - named_adapter) % 4
    ).reshape(1, -1)
    partials = partial_codes(tok, slot, down, far)
    received = lax.all_to_all(partials, "tensor", split_axis=0, concat_axis=0, tiled=True)
    own_codes = jnp.sum(received, axis=0).astype(BF16)
    codes = lax.all_to_all(
        jnp.broadcast_to(own_codes[None], (8,) + own_codes.shape),
        "tensor", split_axis=0, concat_axis=0, tiled=True,
    )

    main, side = tok[256:], tok[:256]
    f1, b1 = both_ways(main, main)
    f2, b2 = both_ways(f1, b1)
    acc, tag = projecting(
        place, None, [(tok, 1), (f1, 0), (b1, 0)], (0, 1, 7), weight, tied=(side,)
    )
    side = tie(side, tag)
    sf1, sb1 = both_ways(side, side)
    f3, b3 = both_ways(f2, b2)
    acc, tag_f, tag_b = projecting(
        place, acc, [(f2, 0), (b2, 0)], (2, 6), weight, tied=(sf1, sb1), after=(partials,)
    )
    sf1, sb1 = tie(sf1, tag_f), tie(sb1, tag_b)
    sf2, sb2 = both_ways(sf1, sb1)
    f4, b4 = both_ways(f3[:512], b3[512:])
    side_acc, tag_f, tag_b = projecting(
        place, None, [(side, 0), (sf1, 0), (sb1, 0)], (0, 1, 7), weight, tied=(sf2, sb2)
    )
    sf2, sb2 = tie(sf2, tag_f), tie(sb2, tag_b)
    sf3, sb3 = both_ways(sf2, sb2)
    mixed, rims = mixing(
        place, acc, (f3, b3), (f4, b4), weight, codes, ids, gathered, taps, 1, (0, 2)
    )
    rim_in = lax.ppermute(rims[1], "seq", [(i, i + 1) for i in range(7)])
    sb4 = moved(sb3, "tensor", -1)
    gated_late = filtering([(mixed, 2, 4)], rims[0], taps, long_filter, skip_row)
    late_pieces = ring(gated_late)
    (side_acc,) = projecting(place, side_acc, [(sf2, 0), (sb2, 0)], (2, 6), weight)
    (side_mixed,) = mixing(
        place, side_acc, (sf3, sb3), (sb4,), weight, codes, ids, gathered, taps, 0, ()
    )
    gated_early = filtering(
        [(side_mixed, 0, 2), (mixed, 0, 2)], rim_in, taps, long_filter, skip_row
    )
    early_pieces = ring(gated_early)
    out = out_projection(late_pieces, gathered, None, 2, rows)
    out = out_projection(early_pieces, gathered, out, 0, rows)
    return out[None]


def solution(mesh):
    return jax.shard_map(
        per_device,
        mesh=mesh,
        in_specs=(
            P("adapter", "seq", "tensor"),
            P(None, None, "tensor"),
            P(("seq", "adapter"), "tensor", None),
            P(("seq", "adapter"), None, None, "tensor"),
            P(None, None, "tensor"),
            P(None, "tensor"),
            P("tensor"),
            P("tensor", None),
            P("adapter", "seq", None),
        ),
        out_specs=P("adapter", "seq", "tensor"),
        check_vma=False,
    )
```

```python
import jax
import jax.numpy as jnp
import numpy as np
from jax import lax
from jax.experimental import pallas as pl
from jax.experimental.pallas import tpu as pltpu
from jax.sharding import PartitionSpec as P

F32 = jnp.float32
BF16 = jnp.bfloat16
PARAMS = pltpu.CompilerParams(vmem_limit_bytes=24 * 1024 * 1024)


def cost(micros):
    return pl.CostEstimate(
        flops=int(micros * 2e9), transcendentals=0, bytes_accessed=int(micros * 2e6)
    )


def in_hbm(array):
    return pltpu.with_memory_space_constraint(array, pltpu.HBM)


def moved(block, axis, distance):
    n = lax.axis_size(axis)
    return lax.ppermute(block, axis, [(i, (i + distance) % n) for i in range(n)])


def nt_dot(a, b):
    return lax.dot_general(a, b, (((1,), (1,)), ((), ())), preferred_element_type=F32)


def codes_kernel(tok_ref, ids_ref, down_ref, *refs):
    out_ref = refs[-1]
    tok = tok_ref[...]
    ids = ids_ref[...]
    total = jnp.zeros((64, tok.shape[0]), F32)
    half = down_ref.shape[0] // 2
    for side in range(2):
        products = nt_dot(down_ref[side * half : (side + 1) * half], tok)
        for own in range(half // 64):
            total = total + jnp.where(
                ids == side * (half // 64) + own, products[own * 64 : own * 64 + 64], 0.0
            )
    for j in range(out_ref.shape[0]):
        out_ref[j] = total[:, 128 * j : 128 * j + 128]


def partial_codes(tok, ids, down, after):
    rows, depth = tok.shape
    block = 256
    return pl.pallas_call(
        codes_kernel,
        grid=(rows // block,),
        in_specs=[
            pl.BlockSpec((block, depth), lambda i: (i, 0)),
            pl.BlockSpec((1, block), lambda i: (0, i)),
            pl.BlockSpec(down.shape, lambda i: (0, 0)),
        ]
        + [pl.BlockSpec(memory_space=pl.ANY) for _ in after],
        out_specs=pl.BlockSpec((block // 128, 64, 128), lambda i: (i, 0, 0)),
        out_shape=jax.ShapeDtypeStruct((rows // 128, 64, 128), F32),
        compiler_params=PARAMS,
        cost_estimate=cost(4.0),
    )(in_hbm(tok), ids, down, *after)


def sum_kernel(parts_ref, *refs):
    out_ref = refs[-1]
    total = parts_ref[0]
    for j in range(1, parts_ref.shape[0]):
        total = total + parts_ref[j]
    total = total.astype(BF16)
    for j in range(out_ref.shape[0]):
        out_ref[j] = total


def summed_codes(parts, after):
    whole = pl.BlockSpec(parts.shape, lambda i: (0, 0, 0))
    return pl.pallas_call(
        sum_kernel,
        grid=(1,),
        in_specs=[whole] + [pl.BlockSpec(memory_space=pl.ANY) for _ in after],
        out_specs=whole,
        out_shape=jax.ShapeDtypeStruct(parts.shape, BF16),
        compiler_params=PARAMS,
        cost_estimate=cost(0.5),
    )(parts, *after)


def weight_spec(weight, k):
    parts, depth, channels = weight.shape
    return pl.BlockSpec(
        (parts, depth // 8, channels), lambda i, place: (0, (place[0] + 8 - k) % 8, 0)
    )


def projecting(place, acc, pieces, ks, weight):
    rows, depth = pieces[0].shape
    block = 256
    parts, _, channels = weight.shape
    width = parts * channels
    old = [] if acc is None else [in_hbm(acc)]
    n = len(pieces)

    def kernel(place_ref, *refs):
        total_in, refs = refs[: len(old)], refs[len(old) :]
        weights, out_ref = refs[n : 2 * n], refs[-1]
        loaded = [piece[...] for piece in refs[:n]]
        for c in range(parts):
            lanes = slice(c * channels, (c + 1) * channels)
            total = jnp.dot(loaded[0], weights[0][c], preferred_element_type=F32)
            for piece, ref in zip(loaded[1:], weights[1:]):
                total = total + jnp.dot(piece, ref[c], preferred_element_type=F32)
            if old:
                total = total + total_in[0][:, lanes]
            out_ref[:, lanes] = total

    acc_spec = pl.BlockSpec((block, width), lambda i, place: (i, 0))
    return pl.pallas_call(
        kernel,
        grid_spec=pltpu.PrefetchScalarGridSpec(
            num_scalar_prefetch=1,
            grid=(rows // block,),
            in_specs=[acc_spec for _ in old]
            + [pl.BlockSpec((block, depth), lambda i, place: (i, 0)) for _ in pieces]
            + [weight_spec(weight, k) for k in ks],
            out_specs=acc_spec,
        ),
        out_shape=jax.ShapeDtypeStruct((rows, width), F32),
        compiler_params=PARAMS,
        cost_estimate=cost(0.0045 * rows),
    )(place, *old, *[in_hbm(piece) for piece in pieces], *[weight for _ in ks])


def mixing(place, acc, last, k, weight, codes, ids, gathered, taps, first_block):
    rows, width = last.shape[0], acc.shape[1]
    block = 256
    steps = rows // block
    depth = last.shape[1]
    channels = width // 3

    def kernel(
        place_ref, acc_ref, last_ref, weight_ref, codes_ref, ids_ref,
        u0_ref, u1_ref, u2_ref, taps_ref, mixed_ref, rim_ref,
    ):
        step = pl.program_id(0)
        packed = codes_ref[...].astype(F32)
        low = jnp.concatenate([packed[j].T for j in range(2)], axis=0).astype(BF16)
        low = jnp.concatenate([low, low], axis=1)
        upper = (lax.broadcasted_iota(jnp.int32, (1, 128), 1) // 64).astype(F32)
        ids_block = jnp.broadcast_to(ids_ref[...].astype(F32), (128, block)).T
        zero = jnp.zeros_like(low)
        spread = jnp.concatenate(
            [jnp.where(ids_block == upper + 2.0 * pair, low, zero) for pair in range(16)], axis=1
        )
        for c, ref in enumerate((u0_ref, u1_ref, u2_ref)):
            lanes = slice(c * channels, (c + 1) * channels)
            total = acc_ref[:, lanes]
            total = total + jnp.dot(last_ref[...], weight_ref[c], preferred_element_type=F32)
            up = ref[...].reshape(-1, channels)
            delta = jnp.dot(spread, up, preferred_element_type=F32).astype(BF16)
            mixed_ref[:, lanes] = (total + delta.astype(F32)).astype(BF16)

        @pl.when(step == steps - 1)
        def _():
            branches = []
            for c in (1, 2):
                lanes = slice(c * channels, (c + 1) * channels)
                tail = mixed_ref[:, lanes].astype(F32)
                running = jnp.zeros((128, channels), F32)
                for tap in range(7):
                    running = (
                        running
                        + taps_ref[c, tap : tap + 1, :] * tail[block - 128 - tap : block - tap]
                    )
                branches.append(running)
            rim_ref[:128] = (branches[0] * branches[1]).astype(BF16)
            for c in range(3):
                rim_ref[128 + 16 * c : 144 + 16 * c] = mixed_ref[
                    block - 16 :, c * channels : (c + 1) * channels
                ]

    def up_spec(c):
        return pl.BlockSpec((32, 64, channels), lambda i, place: (0, c, 0))

    return pl.pallas_call(
        kernel,
        grid_spec=pltpu.PrefetchScalarGridSpec(
            num_scalar_prefetch=1,
            grid=(steps,),
            in_specs=[
                pl.BlockSpec((block, width), lambda i, place: (i + first_block, 0)),
                pl.BlockSpec((block, depth), lambda i, place: (i, 0)),
                weight_spec(weight, k),
                pl.BlockSpec((2, 64, 128), lambda i, place: (i + first_block, 0, 0)),
                pl.BlockSpec((1, block), lambda i, place: (0, i + first_block)),
                up_spec(0),
                up_spec(1),
                up_spec(2),
                pl.BlockSpec(taps.shape, lambda i, place: (0, 0, 0)),
            ],
            out_specs=[
                pl.BlockSpec((block, width), lambda i, place: (i, 0)),
                pl.BlockSpec((176, channels), lambda i, place: (0, 0)),
            ],
        ),
        out_shape=[
            jax.ShapeDtypeStruct((rows, width), BF16),
            jax.ShapeDtypeStruct((176, channels), BF16),
        ],
        compiler_params=PARAMS,
        cost_estimate=cost(4.0),
    )(place, in_hbm(acc), last, weight, codes, ids, *[in_hbm(gathered)] * 3, taps)


def split(array):
    high = array.astype(BF16)
    return high, (array - high.astype(F32)).astype(BF16)


def waves():
    size = 256
    half = size // 2
    k, t = np.arange(half)[:, None], np.arange(size)[None, :]
    angle = 2.0 * np.pi * ((k * t) % size) / size
    cosine, sine = np.cos(angle), np.sin(angle)
    alternating = 1.0 - 2.0 * (np.arange(size) % 2)
    nyquist_first = sine.copy()
    nyquist_first[0] = -alternating
    forward = np.concatenate([cosine, -nyquist_first], 0)
    last = cosine.copy()
    last[0] = alternating
    of_taps = np.concatenate([cosine, -sine, last], 0)[:, :half]
    weights = np.full((half, 1), 2.0 / size)
    weights[0] = 1.0 / size
    inverse = np.concatenate([cosine * weights, -nyquist_first * weights], 0).T[half:]
    return [np.asarray(a, np.float32) for a in (forward, of_taps, inverse)]


def filtering(mixed, rim, taps, spectrum, forward, inverse):
    block = 128
    rows, width = mixed.shape
    channels = width // 3
    steps = rows // block

    def kernel(
        mixed_ref, rim_ref, taps_ref, spectrum_ref, fwd_hi_ref, fwd_lo_ref, inv_hi_ref, inv_lo_ref,
        gated_ref, before_ref, window_ref,
    ):
        step = pl.program_id(0)
        current = mixed_ref[...].astype(F32)

        @pl.when(step == 0)
        def _():
            window_ref[:128] = rim_ref[:128]
            for c in range(3):
                before_ref[:, c * channels : (c + 1) * channels] = rim_ref[
                    128 + 16 * c : 144 + 16 * c
                ].astype(F32)

        @pl.when(step > 0)
        def _():
            window_ref[:128] = window_ref[block:]

        filtered = []
        for c in range(3):
            lanes = slice(c * channels, (c + 1) * channels)
            extended = jnp.concatenate([before_ref[:, lanes], current[:, lanes]], axis=0)
            running = jnp.zeros((block, channels), F32)
            for tap in range(7):
                running = running + taps_ref[c, tap : tap + 1, :] * extended[16 - tap : 16 - tap + block]
            filtered.append(running)
        before_ref[...] = current[block - 16 :]
        window_ref[block:] = (filtered[1] * filtered[2]).astype(BF16)
        window = window_ref[...]
        waves_in = jnp.dot(fwd_hi_ref[...], window, preferred_element_type=F32)
        waves_in = waves_in + jnp.dot(fwd_lo_ref[...], window, preferred_element_type=F32)
        real, imaginary = waves_in[:128], waves_in[128:]
        first, second, third = (spectrum_ref[128 * j : 128 * j + 128] for j in range(3))
        product = jnp.concatenate(
            [real * first - imaginary * second, real * second + imaginary * third], axis=0
        )
        high, low = split(product)
        out = jnp.dot(inv_hi_ref[...], high, preferred_element_type=F32)
        out = out + jnp.dot(inv_hi_ref[...], low, preferred_element_type=F32)
        out = out + jnp.dot(inv_lo_ref[...], high, preferred_element_type=F32)
        gated_ref[...] = (filtered[0] * out).astype(BF16)

    whole = lambda a: pl.BlockSpec(a.shape, lambda i: (0,) * a.ndim)
    operands = [rim, taps, spectrum, *forward, *inverse]
    return pl.pallas_call(
        kernel,
        grid=(steps,),
        in_specs=[pl.BlockSpec((block, width), lambda i: (i, 0))] + [whole(a) for a in operands],
        out_specs=pl.BlockSpec((block, channels), lambda i: (i, 0)),
        out_shape=jax.ShapeDtypeStruct((rows, channels), BF16),
        scratch_shapes=[
            pltpu.VMEM((16, width), F32),
            pltpu.VMEM((256, channels), BF16),
        ],
        compiler_params=PARAMS,
        cost_estimate=cost(3.5),
    )(mixed, *operands)


def out_kernel(*refs):
    pieces, (low_ref, high_ref), out_ref = refs[:8], refs[8:10], refs[-1]
    channels = low_ref.shape[2]
    for side, ref in enumerate((low_ref, high_ref)):
        total = jnp.zeros((out_ref.shape[0], channels), F32)
        for k, piece in zip((0, 1, 7, 2, 6, 3, 5, 4), pieces):
            weight = ref[4 * k : 4 * k + 4].reshape(-1, channels)
            total = total + jnp.dot(piece[...], weight, preferred_element_type=F32)
        out_ref[:, side * channels : (side + 1) * channels] = total.astype(BF16)


def out_projection(pieces, gathered, previous, first_block, rows_all):
    rows, channels = pieces[0].shape
    block = rows // 2
    operands = [in_hbm(a) for a in (*pieces, gathered, gathered)]
    in_specs = (
        [pl.BlockSpec((block, channels), lambda i: (i, 0))] * 8
        + [
            pl.BlockSpec((32, 64, channels), lambda i: (0, 3, 0)),
            pl.BlockSpec((32, 64, channels), lambda i: (0, 4, 0)),
        ]
    )
    aliases = {}
    if previous is not None:
        aliases = {len(operands): 0}
        operands.append(previous)
        in_specs.append(pl.BlockSpec(memory_space=pl.ANY))
    return pl.pallas_call(
        out_kernel,
        grid=(2,),
        in_specs=in_specs,
        out_specs=pl.BlockSpec((block, 2 * channels), lambda i: (i + first_block, 0)),
        out_shape=jax.ShapeDtypeStruct((rows_all, 2 * channels), BF16),
        input_output_aliases=aliases,
        compiler_params=PARAMS,
        cost_estimate=cost(2.3),
    )(*operands)


def parcel_kernel(up_ref, rows_ref, out_ref):
    height, channels = up_ref.shape
    out_ref[:height] = up_ref[...]
    depth = rows_ref.shape[0]
    out_ref[height : height + depth] = rows_ref[:, :channels]
    out_ref[height + depth :] = rows_ref[:, channels:]


def parcel(up, rows):
    height = up.shape[0] + 2 * rows.shape[0]
    return pl.pallas_call(
        parcel_kernel,
        grid=(1,),
        in_specs=[
            pl.BlockSpec(up.shape, lambda i: (0, 0)),
            pl.BlockSpec(rows.shape, lambda i: (0, 0)),
        ],
        out_specs=pl.BlockSpec((height, up.shape[1]), lambda i: (0, 0)),
        out_shape=jax.ShapeDtypeStruct((height, up.shape[1]), BF16),
        compiler_params=PARAMS,
        cost_estimate=cost(0.5),
    )(up, rows)


def both_ways(ahead, back):
    return moved(ahead, "tensor", 1), moved(back, "tensor", -1)


def ring(block, last):
    ahead = back = block
    pieces = [block]
    for _ in range(3):
        ahead, back = both_ways(ahead, back)
        pieces += [ahead, back]
    return pieces + [moved(ahead if last > 0 else back, "tensor", last)]


def per_device(
    tokens,
    in_weight,
    adapter_down_maps,
    adapter_up_maps,
    short_filter,
    long_filter,
    skip,
    out_weight,
    adapter_ids,
):
    tok = tokens[0]
    ids = adapter_ids.reshape(1, -1)
    rows, depth = tok.shape
    channels = in_weight.shape[2]
    rank = adapter_down_maps.shape[2]
    seq, tensor, adapter = (lax.axis_index(name) for name in ("seq", "tensor", "adapter"))
    place = tensor.astype(jnp.int32).reshape(1)
    weight = in_hbm(in_weight.transpose(1, 0, 2))
    taps = short_filter.transpose(1, 0, 2)

    half = rows // 2
    f1, b1 = both_ways(tok, tok)
    f2, b2 = both_ways(f1, b1)
    f3, b3 = both_ways(f2, b2)
    f4, b4 = both_ways(f3[half:], b3[:half])

    acc = projecting(place, None, (tok, f1, b1), (0, 1, 7), weight)
    down_all = lax.all_to_all(
        jnp.broadcast_to(adapter_down_maps[0].T[None], (32, rank, depth)),
        ("seq", "adapter"), split_axis=0, concat_axis=0, tiled=True,
    )
    forward, of_taps, inverse = (jnp.asarray(a) for a in waves())
    spectrum = jnp.dot(
        of_taps, long_filter.at[0].add(skip), precision=lax.Precision.HIGHEST
    )
    partials = partial_codes(tok, ids, down_all.reshape(-1, depth), (acc, spectrum, f2, b2))
    received = lax.all_to_all(partials, "tensor", split_axis=0, concat_axis=0, tiled=True)
    acc = projecting(place, acc, (f2, b2), (2, 6), weight)
    codes = lax.all_to_all(
        summed_codes(received, (acc, f3, b3)), "tensor", split_axis=0, concat_axis=0, tiled=True
    )

    acc = projecting(place, acc, (f3, b3), (3, 5), weight)
    quarter = out_weight.shape[0] // 4
    out_rows = lax.dynamic_slice(
        out_weight,
        (adapter * quarter, ((tensor + seq) % 8) * depth),
        (quarter, depth),
    )
    out_rows = lax.ppermute(
        out_rows,
        ("seq", "tensor"),
        [(s * 8 + z, s * 8 + (z + s) % 8) for s in range(8) for z in range(8)],
    )
    up = adapter_up_maps[0].transpose(1, 0, 2).reshape(-1, channels)
    gathered = lax.all_gather(parcel(up, out_rows), ("seq", "adapter"), axis=0)

    shared = (weight, codes, ids, gathered, taps)
    mixed_late, rim_late = mixing(place, acc, f4, 4, *shared, half // 256)
    rim_in = lax.ppermute(rim_late, "seq", [(i, i + 1) for i in range(7)])
    mixed_early, rim_early = mixing(place, acc, b4, 4, *shared, 0)

    filters = (taps, spectrum, split(forward), split(inverse))
    gated_early = ring(filtering(mixed_early, rim_in, *filters), 1)
    gated_late = ring(filtering(mixed_late, rim_early, *filters), -1)
    out = out_projection(gated_early, gathered, None, 0, rows)
    out = out_projection(gated_late, gathered, out, 2, rows)
    return out[None]


def solution(mesh):
    return jax.shard_map(
        per_device,
        mesh=mesh,
        in_specs=(
            P("adapter", "seq", "tensor"),
            P(None, None, "tensor"),
            P(("seq", "adapter"), "tensor", None),
            P(("seq", "adapter"), None, None, "tensor"),
            P(None, None, "tensor"),
            P(None, "tensor"),
            P("tensor"),
            P("tensor", None),
            P("adapter", "seq", None),
        ),
        out_specs=P("adapter", "seq", "tensor"),
        check_vma=False,
    )
```

```python
import jax
import jax.numpy as jnp
import numpy as np
from jax import lax
from jax.experimental import pallas as pl
from jax.experimental.pallas import tpu as pltpu
from jax.sharding import PartitionSpec as P

F32 = jnp.float32
BF16 = jnp.bfloat16
PARAMS = pltpu.CompilerParams(vmem_limit_bytes=24 * 1024 * 1024)


def cost(micros):
    return pl.CostEstimate(
        flops=int(micros * 2e9), transcendentals=0, bytes_accessed=int(micros * 2e6)
    )


def in_hbm(array):
    return pltpu.with_memory_space_constraint(array, pltpu.HBM)


def moved(block, axis, distance):
    n = lax.axis_size(axis)
    return lax.ppermute(block, axis, [(i, (i + distance) % n) for i in range(n)])


def nt_dot(a, b):
    return lax.dot_general(a, b, (((1,), (1,)), ((), ())), preferred_element_type=F32)


def codes_kernel(tok_ref, ids_ref, down_ref, *refs):
    out_ref = refs[-1]
    tok = tok_ref[...]
    ids = ids_ref[...]
    total = jnp.zeros((64, tok.shape[0]), F32)
    half = down_ref.shape[0] // 2
    for side in range(2):
        products = nt_dot(down_ref[side * half : (side + 1) * half], tok)
        for own in range(half // 64):
            total = total + jnp.where(
                ids == side * (half // 64) + own, products[own * 64 : own * 64 + 64], 0.0
            )
    for j in range(out_ref.shape[0]):
        out_ref[j] = total[:, 128 * j : 128 * j + 128]


def partial_codes(tok, ids, down, after):
    rows, depth = tok.shape
    block = 256
    return pl.pallas_call(
        codes_kernel,
        grid=(rows // block,),
        in_specs=[
            pl.BlockSpec((block, depth), lambda i: (i, 0)),
            pl.BlockSpec((1, block), lambda i: (0, i)),
            pl.BlockSpec(down.shape, lambda i: (0, 0)),
        ]
        + [pl.BlockSpec(memory_space=pl.ANY) for _ in after],
        out_specs=pl.BlockSpec((block // 128, 64, 128), lambda i: (i, 0, 0)),
        out_shape=jax.ShapeDtypeStruct((rows // 128, 64, 128), F32),
        compiler_params=PARAMS,
        cost_estimate=cost(4.0),
    )(in_hbm(tok), ids, down, *[in_hbm(a) for a in after])


def sum_kernel(parts_ref, *refs):
    out_ref = refs[-1]
    total = parts_ref[0]
    for j in range(1, parts_ref.shape[0]):
        total = total + parts_ref[j]
    total = total.astype(BF16)
    for j in range(out_ref.shape[0]):
        out_ref[j] = total


def summed_codes(parts, after):
    whole = pl.BlockSpec(parts.shape, lambda i: (0, 0, 0))
    return pl.pallas_call(
        sum_kernel,
        grid=(1,),
        in_specs=[whole] + [pl.BlockSpec(memory_space=pl.ANY) for _ in after],
        out_specs=whole,
        out_shape=jax.ShapeDtypeStruct(parts.shape, BF16),
        compiler_params=PARAMS,
        cost_estimate=cost(0.5),
    )(parts, *[in_hbm(a) for a in after])


def weight_spec(weight, k):
    parts, depth, channels = weight.shape
    return pl.BlockSpec(
        (parts, depth // 8, channels), lambda i, place: (0, (place[0] + 8 - k) % 8, 0)
    )


def projecting(place, acc, pieces, ks, weight):
    rows, depth = pieces[0].shape
    block = 256
    parts, _, channels = weight.shape
    width = parts * channels
    old = [] if acc is None else [in_hbm(acc)]
    n = len(pieces)

    def kernel(place_ref, *refs):
        total_in, refs = refs[: len(old)], refs[len(old) :]
        weights, out_ref = refs[n : 2 * n], refs[-1]
        loaded = [piece[...] for piece in refs[:n]]
        for c in range(parts):
            lanes = slice(c * channels, (c + 1) * channels)
            total = jnp.dot(loaded[0], weights[0][c], preferred_element_type=F32)
            for piece, ref in zip(loaded[1:], weights[1:]):
                total = total + jnp.dot(piece, ref[c], preferred_element_type=F32)
            if old:
                total = total + total_in[0][:, lanes]
            out_ref[:, lanes] = total

    acc_spec = pl.BlockSpec((block, width), lambda i, place: (i, 0))
    return pl.pallas_call(
        kernel,
        grid_spec=pltpu.PrefetchScalarGridSpec(
            num_scalar_prefetch=1,
            grid=(rows // block,),
            in_specs=[acc_spec for _ in old]
            + [pl.BlockSpec((block, depth), lambda i, place: (i, 0)) for _ in pieces]
            + [weight_spec(weight, k) for k in ks],
            out_specs=acc_spec,
        ),
        out_shape=jax.ShapeDtypeStruct((rows, width), F32),
        compiler_params=PARAMS,
        cost_estimate=cost(0.0045 * rows),
    )(place, *old, *[in_hbm(piece) for piece in pieces], *[weight for _ in ks])


def mixing(place, acc, last, k, weight, codes, ids, gathered, taps, first_block):
    rows, width = last.shape[0], acc.shape[1]
    block = 256
    steps = rows // block
    depth = last.shape[1]
    channels = width // 3

    def kernel(
        place_ref, acc_ref, last_ref, weight_ref, codes_ref, ids_ref,
        u0_ref, u1_ref, u2_ref, taps_ref, mixed_ref, rim_ref,
    ):
        step = pl.program_id(0)
        packed = codes_ref[...].astype(F32)
        low = jnp.concatenate([packed[j].T for j in range(2)], axis=0).astype(BF16)
        low = jnp.concatenate([low, low], axis=1)
        upper = (lax.broadcasted_iota(jnp.int32, (1, 128), 1) // 64).astype(F32)
        ids_block = jnp.broadcast_to(ids_ref[...].astype(F32), (128, block)).T
        zero = jnp.zeros_like(low)
        spread = jnp.concatenate(
            [jnp.where(ids_block == upper + 2.0 * pair, low, zero) for pair in range(16)], axis=1
        )
        for c, ref in enumerate((u0_ref, u1_ref, u2_ref)):
            lanes = slice(c * channels, (c + 1) * channels)
            total = acc_ref[:, lanes]
            total = total + jnp.dot(last_ref[...], weight_ref[c], preferred_element_type=F32)
            up = ref[...].reshape(-1, channels)
            delta = jnp.dot(spread, up, preferred_element_type=F32).astype(BF16)
            mixed_ref[:, lanes] = (total + delta.astype(F32)).astype(BF16)

        @pl.when(step == steps - 1)
        def _():
            branches = []
            for c in (1, 2):
                lanes = slice(c * channels, (c + 1) * channels)
                tail = mixed_ref[:, lanes].astype(F32)
                running = jnp.zeros((128, channels), F32)
                for tap in range(7):
                    running = (
                        running
                        + taps_ref[c, tap : tap + 1, :] * tail[block - 128 - tap : block - tap]
                    )
                branches.append(running)
            rim_ref[:128] = (branches[0] * branches[1]).astype(BF16)
            for c in range(3):
                rim_ref[128 + 16 * c : 144 + 16 * c] = mixed_ref[
                    block - 16 :, c * channels : (c + 1) * channels
                ]

    def up_spec(c):
        return pl.BlockSpec((32, 64, channels), lambda i, place: (0, c, 0))

    return pl.pallas_call(
        kernel,
        grid_spec=pltpu.PrefetchScalarGridSpec(
            num_scalar_prefetch=1,
            grid=(steps,),
            in_specs=[
                pl.BlockSpec((block, width), lambda i, place: (i + first_block, 0)),
                pl.BlockSpec((block, depth), lambda i, place: (i, 0)),
                weight_spec(weight, k),
                pl.BlockSpec((2, 64, 128), lambda i, place: (i + first_block, 0, 0)),
                pl.BlockSpec((1, block), lambda i, place: (0, i + first_block)),
                up_spec(0),
                up_spec(1),
                up_spec(2),
                pl.BlockSpec(taps.shape, lambda i, place: (0, 0, 0)),
            ],
            out_specs=[
                pl.BlockSpec((block, width), lambda i, place: (i, 0)),
                pl.BlockSpec((176, channels), lambda i, place: (0, 0)),
            ],
        ),
        out_shape=[
            jax.ShapeDtypeStruct((rows, width), BF16),
            jax.ShapeDtypeStruct((176, channels), BF16),
        ],
        compiler_params=PARAMS,
        cost_estimate=cost(4.0),
    )(place, in_hbm(acc), last, weight, codes, ids, *[in_hbm(gathered)] * 3, taps)


def split(array):
    high = array.astype(BF16)
    return high, (array - high.astype(F32)).astype(BF16)


def waves():
    size = 256
    half = size // 2
    k, t = np.arange(half)[:, None], np.arange(size)[None, :]
    angle = 2.0 * np.pi * ((k * t) % size) / size
    cosine, sine = np.cos(angle), np.sin(angle)
    alternating = 1.0 - 2.0 * (np.arange(size) % 2)
    nyquist_first = sine.copy()
    nyquist_first[0] = -alternating
    forward = np.concatenate([cosine, -nyquist_first], 0)
    last = cosine.copy()
    last[0] = alternating
    of_taps = np.concatenate([cosine, -sine, last], 0)[:, :half]
    weights = np.full((half, 1), 2.0 / size)
    weights[0] = 1.0 / size
    inverse = np.concatenate([cosine * weights, -nyquist_first * weights], 0).T[half:]
    return [np.asarray(a, np.float32) for a in (forward, of_taps, inverse)]


def filtering(mixed, rim, taps, spectrum, forward, inverse):
    block = 128
    rows, width = mixed.shape
    channels = width // 3
    steps = rows // block

    def kernel(
        mixed_ref, rim_ref, taps_ref, spectrum_ref, fwd_hi_ref, fwd_lo_ref, inv_hi_ref, inv_lo_ref,
        gated_ref, before_ref, window_ref,
    ):
        step = pl.program_id(0)
        current = mixed_ref[...].astype(F32)

        @pl.when(step == 0)
        def _():
            window_ref[:128] = rim_ref[:128]
            for c in range(3):
                before_ref[:, c * channels : (c + 1) * channels] = rim_ref[
                    128 + 16 * c : 144 + 16 * c
                ].astype(F32)

        @pl.when(step > 0)
        def _():
            window_ref[:128] = window_ref[block:]

        filtered = []
        for c in range(3):
            lanes = slice(c * channels, (c + 1) * channels)
            extended = jnp.concatenate([before_ref[:, lanes], current[:, lanes]], axis=0)
            running = jnp.zeros((block, channels), F32)
            for tap in range(7):
                running = running + taps_ref[c, tap : tap + 1, :] * extended[16 - tap : 16 - tap + block]
            filtered.append(running)
        before_ref[...] = current[block - 16 :]
        window_ref[block:] = (filtered[1] * filtered[2]).astype(BF16)
        window = window_ref[...]
        waves_in = jnp.dot(fwd_hi_ref[...], window, preferred_element_type=F32)
        waves_in = waves_in + jnp.dot(fwd_lo_ref[...], window, preferred_element_type=F32)
        real, imaginary = waves_in[:128], waves_in[128:]
        first, second, third = (spectrum_ref[128 * j : 128 * j + 128] for j in range(3))
        product = jnp.concatenate(
            [real * first - imaginary * second, real * second + imaginary * third], axis=0
        )
        high, low = split(product)
        out = jnp.dot(inv_hi_ref[...], high, preferred_element_type=F32)
        out = out + jnp.dot(inv_hi_ref[...], low, preferred_element_type=F32)
        out = out + jnp.dot(inv_lo_ref[...], high, preferred_element_type=F32)
        gated_ref[...] = (filtered[0] * out).astype(BF16)

    whole = lambda a: pl.BlockSpec(a.shape, lambda i: (0,) * a.ndim)
    operands = [rim, taps, spectrum, *forward, *inverse]
    return pl.pallas_call(
        kernel,
        grid=(steps,),
        in_specs=[pl.BlockSpec((block, width), lambda i: (i, 0))] + [whole(a) for a in operands],
        out_specs=pl.BlockSpec((block, channels), lambda i: (i, 0)),
        out_shape=jax.ShapeDtypeStruct((rows, channels), BF16),
        scratch_shapes=[
            pltpu.VMEM((16, width), F32),
            pltpu.VMEM((256, channels), BF16),
        ],
        compiler_params=PARAMS,
        cost_estimate=cost(3.5),
    )(mixed, *operands)


def out_kernel(*refs):
    pieces, (low_ref, high_ref), out_ref = refs[:8], refs[8:10], refs[-1]
    channels = low_ref.shape[2]
    for side, ref in enumerate((low_ref, high_ref)):
        total = jnp.zeros((out_ref.shape[0], channels), F32)
        for k, piece in zip((0, 1, 7, 2, 6, 3, 5, 4), pieces):
            weight = ref[4 * k : 4 * k + 4].reshape(-1, channels)
            total = total + jnp.dot(piece[...], weight, preferred_element_type=F32)
        out_ref[:, side * channels : (side + 1) * channels] = total.astype(BF16)


def out_projection(pieces, gathered, previous, first_block, rows_all):
    rows, channels = pieces[0].shape
    block = rows // 2
    operands = [*pieces, in_hbm(gathered), in_hbm(gathered)]
    in_specs = (
        [pl.BlockSpec((block, channels), lambda i: (i, 0))] * 8
        + [
            pl.BlockSpec((32, 64, channels), lambda i: (0, 0, 0)),
            pl.BlockSpec((32, 64, channels), lambda i: (0, 1, 0)),
        ]
    )
    aliases = {}
    if previous is not None:
        aliases = {len(operands): 0}
        operands.append(previous)
        in_specs.append(pl.BlockSpec(memory_space=pl.ANY))
    return pl.pallas_call(
        out_kernel,
        grid=(2,),
        in_specs=in_specs,
        out_specs=pl.BlockSpec((block, 2 * channels), lambda i: (i + first_block, 0)),
        out_shape=jax.ShapeDtypeStruct((rows_all, 2 * channels), BF16),
        input_output_aliases=aliases,
        compiler_params=PARAMS,
        cost_estimate=cost(2.3),
    )(*operands)


def halves_kernel(ahead_ref, back_ref, ahead_out_ref, back_out_ref):
    ahead_out_ref[...] = ahead_ref[...]
    back_out_ref[...] = back_ref[...]


def halves(ahead, back):
    rows, depth = ahead.shape
    block = rows // 4
    return pl.pallas_call(
        halves_kernel,
        grid=(2,),
        in_specs=[
            pl.BlockSpec((block, depth), lambda i: (i + 2, 0)),
            pl.BlockSpec((block, depth), lambda i: (i, 0)),
        ],
        out_specs=[pl.BlockSpec((block, depth), lambda i: (i, 0))] * 2,
        out_shape=[jax.ShapeDtypeStruct((rows // 2, depth), BF16)] * 2,
        compiler_params=PARAMS,
        cost_estimate=cost(0.5),
    )(in_hbm(ahead), in_hbm(back))


def folding_kernel(rows_ref, after_ref, more_ref, out_ref):
    depth, width = rows_ref.shape
    out_ref[:depth] = rows_ref[:, : width // 2]
    out_ref[depth:] = rows_ref[:, width // 2 :]


def folded(rows, after, more):
    depth, width = rows.shape
    shape = (2 * depth, width // 2)
    return pl.pallas_call(
        folding_kernel,
        grid=(1,),
        in_specs=[
            pl.BlockSpec(rows.shape, lambda i: (0, 0)),
            pl.BlockSpec(memory_space=pl.ANY),
            pl.BlockSpec(memory_space=pl.ANY),
        ],
        out_specs=pl.BlockSpec(shape, lambda i: (0, 0)),
        out_shape=jax.ShapeDtypeStruct(shape, BF16),
        compiler_params=PARAMS,
        cost_estimate=cost(0.5),
    )(rows, in_hbm(after), in_hbm(more))


def both_ways(ahead, back):
    return moved(ahead, "tensor", 1), moved(back, "tensor", -1)


def ring(block, last):
    ahead = back = block
    pieces = [block]
    for _ in range(3):
        ahead, back = both_ways(ahead, back)
        pieces += [ahead, back]
    return pieces + [moved(ahead if last > 0 else back, "tensor", last)]


def per_device(
    tokens,
    in_weight,
    adapter_down_maps,
    adapter_up_maps,
    short_filter,
    long_filter,
    skip,
    out_weight,
    adapter_ids,
):
    tok = tokens[0]
    ids = adapter_ids.reshape(1, -1)
    rows, depth = tok.shape
    channels = in_weight.shape[2]
    rank = adapter_down_maps.shape[2]
    seq, tensor, adapter = (lax.axis_index(name) for name in ("seq", "tensor", "adapter"))
    place = tensor.astype(jnp.int32).reshape(1)
    weight = in_hbm(in_weight.transpose(1, 0, 2))
    taps = short_filter.transpose(1, 0, 2)

    half = rows // 2
    f1, b1 = both_ways(tok, tok)
    f2, b2 = both_ways(f1, b1)
    f3, b3 = both_ways(f2, b2)
    f3_half, b3_half = halves(f3, b3)
    f4, b4 = both_ways(f3_half, b3_half)

    up = adapter_up_maps[0].transpose(1, 0, 2).reshape(-1, channels)
    up_all = lax.all_gather(up, ("seq", "adapter"), axis=0)
    acc = first_acc = projecting(place, None, (tok, f1, b1), (0, 1, 7), weight)
    down_all = lax.all_to_all(
        jnp.broadcast_to(adapter_down_maps[0].T[None], (32, rank, depth)),
        ("seq", "adapter"), split_axis=0, concat_axis=0, tiled=True,
    )
    forward, of_taps, inverse = (jnp.asarray(a) for a in waves())
    spectrum = jnp.dot(
        of_taps, long_filter.at[0].add(skip), precision=lax.Precision.HIGHEST
    )
    partials = partial_codes(tok, ids, down_all.reshape(-1, depth), (acc, f2, b2))
    received = lax.all_to_all(partials, "tensor", split_axis=0, concat_axis=0, tiled=True)
    acc = projecting(place, acc, (f2, b2), (2, 6), weight)
    codes = lax.all_to_all(
        summed_codes(received, (acc, f3_half, b3_half)), "tensor", split_axis=0, concat_axis=0, tiled=True
    )

    acc = projecting(place, acc, (f3, b3), (3, 5), weight)
    quarter = out_weight.shape[0] // 4
    out_rows = lax.dynamic_slice(
        out_weight,
        (adapter * quarter, ((tensor + seq) % 8) * depth),
        (quarter, depth),
    )
    out_rows = lax.ppermute(
        folded(out_rows, first_acc, spectrum),
        ("seq", "tensor"),
        [(s * 8 + z, s * 8 + (z + s) % 8) for s in range(8) for z in range(8)],
    )
    out_all = lax.all_gather(out_rows, ("seq", "adapter"), axis=0)

    shared = (weight, codes, ids, up_all, taps)
    mixed_late, rim_late = mixing(place, acc, f4, 4, *shared, half // 256)
    rim_in = lax.ppermute(rim_late, "seq", [(i, i + 1) for i in range(7)])
    mixed_early, rim_early = mixing(place, acc, b4, 4, *shared, 0)

    filters = (taps, spectrum, split(forward), split(inverse))
    gated_early = ring(filtering(mixed_early, rim_in, *filters), 1)
    gated_late = ring(filtering(mixed_late, rim_early, *filters), -1)
    out = out_projection(gated_early, out_all, None, 0, rows)
    out = out_projection(gated_late, out_all, out, 2, rows)
    return out[None]


def solution(mesh):
    return jax.shard_map(
        per_device,
        mesh=mesh,
        in_specs=(
            P("adapter", "seq", "tensor"),
            P(None, None, "tensor"),
            P(("seq", "adapter"), "tensor", None),
            P(("seq", "adapter"), None, None, "tensor"),
            P(None, None, "tensor"),
            P(None, "tensor"),
            P("tensor"),
            P("tensor", None),
            P("adapter", "seq", None),
        ),
        out_specs=P("adapter", "seq", "tensor"),
        check_vma=False,
    )
```

```python
import jax
import jax.numpy as jnp
import numpy as np
from jax import lax
from jax.experimental import pallas as pl
from jax.experimental.pallas import tpu as pltpu
from jax.sharding import PartitionSpec as P

F32 = jnp.float32
BF16 = jnp.bfloat16
PARAMS = pltpu.CompilerParams(vmem_limit_bytes=24 * 1024 * 1024)


def cost(micros):
    return pl.CostEstimate(
        flops=int(micros * 2e9), transcendentals=0, bytes_accessed=int(micros * 2e6)
    )


def in_hbm(array):
    return pltpu.with_memory_space_constraint(array, pltpu.HBM)


def moved(block, axis, distance):
    n = lax.axis_size(axis)
    return lax.ppermute(block, axis, [(i, (i + distance) % n) for i in range(n)])


def nt_dot(a, b):
    return lax.dot_general(a, b, (((1,), (1,)), ((), ())), preferred_element_type=F32)


def codes_kernel(tok_ref, ids_ref, down_ref, *refs):
    out_ref = refs[-1]
    tok = tok_ref[...]
    ids = ids_ref[...]
    total = jnp.zeros((64, tok.shape[0]), F32)
    half = down_ref.shape[0] // 2
    for side in range(2):
        products = nt_dot(down_ref[side * half : (side + 1) * half], tok)
        for own in range(half // 64):
            total = total + jnp.where(
                ids == side * (half // 64) + own, products[own * 64 : own * 64 + 64], 0.0
            )
    for j in range(out_ref.shape[0]):
        out_ref[j] = total[:, 128 * j : 128 * j + 128].astype(BF16)


def partial_codes(tok, ids, down, after):
    rows, depth = tok.shape
    block = 256
    return pl.pallas_call(
        codes_kernel,
        grid=(rows // block,),
        in_specs=[
            pl.BlockSpec((block, depth), lambda i: (i, 0)),
            pl.BlockSpec((1, block), lambda i: (0, i)),
            pl.BlockSpec(down.shape, lambda i: (0, 0)),
        ]
        + [pl.BlockSpec(memory_space=pl.ANY) for _ in after],
        out_specs=pl.BlockSpec((block // 128, 64, 128), lambda i: (i, 0, 0)),
        out_shape=jax.ShapeDtypeStruct((rows // 128, 64, 128), BF16),
        compiler_params=PARAMS,
        cost_estimate=cost(4.0),
    )(in_hbm(tok), ids, down, *[in_hbm(a) for a in after])


def sum_kernel(parts_ref, *refs):
    out_ref = refs[-1]
    total = parts_ref[0].astype(F32)
    for j in range(1, parts_ref.shape[0]):
        total = total + parts_ref[j].astype(F32)
    total = total.astype(BF16)
    for j in range(out_ref.shape[0]):
        out_ref[j] = total


def summed_codes(parts, after):
    whole = pl.BlockSpec(parts.shape, lambda i: (0, 0, 0))
    return pl.pallas_call(
        sum_kernel,
        grid=(1,),
        in_specs=[whole] + [pl.BlockSpec(memory_space=pl.ANY) for _ in after],
        out_specs=whole,
        out_shape=jax.ShapeDtypeStruct(parts.shape, BF16),
        compiler_params=PARAMS,
        cost_estimate=cost(0.5),
    )(parts, *[in_hbm(a) for a in after])


def weight_spec(weight, k):
    parts, depth, channels = weight.shape
    return pl.BlockSpec(
        (parts, depth // 8, channels), lambda i, place: (0, (place[0] + 8 - k) % 8, 0)
    )


def projecting(place, acc, pieces, ks, weight):
    rows, depth = pieces[0].shape
    block = 256
    parts, _, channels = weight.shape
    width = parts * channels
    old = [] if acc is None else [in_hbm(acc)]
    n = len(pieces)

    def kernel(place_ref, *refs):
        total_in, refs = refs[: len(old)], refs[len(old) :]
        weights, out_ref = refs[n : 2 * n], refs[-1]
        loaded = [piece[...] for piece in refs[:n]]
        for c in range(parts):
            lanes = slice(c * channels, (c + 1) * channels)
            total = jnp.dot(loaded[0], weights[0][c], preferred_element_type=F32)
            for piece, ref in zip(loaded[1:], weights[1:]):
                total = total + jnp.dot(piece, ref[c], preferred_element_type=F32)
            if old:
                total = total + total_in[0][:, lanes]
            out_ref[:, lanes] = total

    acc_spec = pl.BlockSpec((block, width), lambda i, place: (i, 0))
    return pl.pallas_call(
        kernel,
        grid_spec=pltpu.PrefetchScalarGridSpec(
            num_scalar_prefetch=1,
            grid=(rows // block,),
            in_specs=[acc_spec for _ in old]
            + [pl.BlockSpec((block, depth), lambda i, place: (i, 0)) for _ in pieces]
            + [weight_spec(weight, k) for k in ks],
            out_specs=acc_spec,
        ),
        out_shape=jax.ShapeDtypeStruct((rows, width), F32),
        compiler_params=PARAMS,
        cost_estimate=cost(0.0045 * rows),
    )(place, *old, *[in_hbm(piece) for piece in pieces], *[weight for _ in ks])


def mixing(place, acc, last, k, weight, codes, ids, gathered, taps, first_block):
    rows, width = last.shape[0], acc.shape[1]
    block = 256
    steps = rows // block
    depth = last.shape[1]
    channels = width // 3

    def kernel(
        place_ref, acc_ref, last_ref, weight_ref, codes_ref, ids_ref,
        u0_ref, u1_ref, u2_ref, taps_ref, mixed_ref, rim_ref,
    ):
        step = pl.program_id(0)
        packed = codes_ref[...].astype(F32)
        low = jnp.concatenate([packed[j].T for j in range(2)], axis=0).astype(BF16)
        low = jnp.concatenate([low, low], axis=1)
        upper = (lax.broadcasted_iota(jnp.int32, (1, 128), 1) // 64).astype(F32)
        ids_block = jnp.broadcast_to(ids_ref[...].astype(F32), (128, block)).T
        zero = jnp.zeros_like(low)
        spread = jnp.concatenate(
            [jnp.where(ids_block == upper + 2.0 * pair, low, zero) for pair in range(16)], axis=1
        )
        for c, ref in enumerate((u0_ref, u1_ref, u2_ref)):
            lanes = slice(c * channels, (c + 1) * channels)
            total = acc_ref[:, lanes]
            total = total + jnp.dot(last_ref[...], weight_ref[c], preferred_element_type=F32)
            up = ref[...].reshape(-1, channels)
            delta = jnp.dot(spread, up, preferred_element_type=F32).astype(BF16)
            mixed_ref[:, lanes] = (total + delta.astype(F32)).astype(BF16)

        @pl.when(step == steps - 1)
        def _():
            branches = []
            for c in (1, 2):
                lanes = slice(c * channels, (c + 1) * channels)
                tail = mixed_ref[:, lanes].astype(F32)
                running = jnp.zeros((128, channels), F32)
                for tap in range(7):
                    running = (
                        running
                        + taps_ref[c, tap : tap + 1, :] * tail[block - 128 - tap : block - tap]
                    )
                branches.append(running)
            rim_ref[:128] = (branches[0] * branches[1]).astype(BF16)
            for c in range(3):
                rim_ref[128 + 16 * c : 144 + 16 * c] = mixed_ref[
                    block - 16 :, c * channels : (c + 1) * channels
                ]

    def up_spec(c):
        return pl.BlockSpec((32, 64, channels), lambda i, place: (0, c, 0))

    return pl.pallas_call(
        kernel,
        grid_spec=pltpu.PrefetchScalarGridSpec(
            num_scalar_prefetch=1,
            grid=(steps,),
            in_specs=[
                pl.BlockSpec((block, width), lambda i, place: (i + first_block, 0)),
                pl.BlockSpec((block, depth), lambda i, place: (i, 0)),
                weight_spec(weight, k),
                pl.BlockSpec((2, 64, 128), lambda i, place: (i + first_block, 0, 0)),
                pl.BlockSpec((1, block), lambda i, place: (0, i + first_block)),
                up_spec(0),
                up_spec(1),
                up_spec(2),
                pl.BlockSpec(taps.shape, lambda i, place: (0, 0, 0)),
            ],
            out_specs=[
                pl.BlockSpec((block, width), lambda i, place: (i, 0)),
                pl.BlockSpec((176, channels), lambda i, place: (0, 0)),
            ],
        ),
        out_shape=[
            jax.ShapeDtypeStruct((rows, width), BF16),
            jax.ShapeDtypeStruct((176, channels), BF16),
        ],
        compiler_params=PARAMS,
        cost_estimate=cost(4.0),
    )(place, in_hbm(acc), last, weight, codes, ids, *[in_hbm(gathered)] * 3, taps)


def split(array):
    high = array.astype(BF16)
    return high, (array - high.astype(F32)).astype(BF16)


def waves():
    size = 256
    half = size // 2
    k, t = np.arange(half)[:, None], np.arange(size)[None, :]
    angle = 2.0 * np.pi * ((k * t) % size) / size
    cosine, sine = np.cos(angle), np.sin(angle)
    alternating = 1.0 - 2.0 * (np.arange(size) % 2)
    nyquist_first = sine.copy()
    nyquist_first[0] = -alternating
    forward = np.concatenate([cosine, -nyquist_first], 0)
    last = cosine.copy()
    last[0] = alternating
    of_taps = np.concatenate([cosine, -sine, last], 0)[:, :half]
    weights = np.full((half, 1), 2.0 / size)
    weights[0] = 1.0 / size
    inverse = np.concatenate([cosine * weights, -nyquist_first * weights], 0).T[half:]
    return [np.asarray(a, np.float32) for a in (forward, of_taps, inverse)]


def filtering(mixed, rim, taps, spectrum, forward, inverse):
    block = 128
    rows, width = mixed.shape
    channels = width // 3
    steps = rows // block

    def kernel(
        mixed_ref, rim_ref, taps_ref, spectrum_ref, fwd_hi_ref, fwd_lo_ref, inv_hi_ref, inv_lo_ref,
        gated_ref, before_ref, window_ref,
    ):
        step = pl.program_id(0)
        current = mixed_ref[...].astype(F32)

        @pl.when(step == 0)
        def _():
            window_ref[:128] = rim_ref[:128]
            for c in range(3):
                before_ref[:, c * channels : (c + 1) * channels] = rim_ref[
                    128 + 16 * c : 144 + 16 * c
                ].astype(F32)

        @pl.when(step > 0)
        def _():
            window_ref[:128] = window_ref[block:]

        filtered = []
        for c in range(3):
            lanes = slice(c * channels, (c + 1) * channels)
            extended = jnp.concatenate([before_ref[:, lanes], current[:, lanes]], axis=0)
            running = jnp.zeros((block, channels), F32)
            for tap in range(7):
                running = running + taps_ref[c, tap : tap + 1, :] * extended[16 - tap : 16 - tap + block]
            filtered.append(running)
        before_ref[...] = current[block - 16 :]
        window_ref[block:] = (filtered[1] * filtered[2]).astype(BF16)
        window = window_ref[...]
        waves_in = jnp.dot(fwd_hi_ref[...], window, preferred_element_type=F32)
        waves_in = waves_in + jnp.dot(fwd_lo_ref[...], window, preferred_element_type=F32)
        real, imaginary = waves_in[:128], waves_in[128:]
        first, second, third = (spectrum_ref[128 * j : 128 * j + 128] for j in range(3))
        product = jnp.concatenate(
            [real * first - imaginary * second, real * second + imaginary * third], axis=0
        )
        high, low = split(product)
        out = jnp.dot(inv_hi_ref[...], high, preferred_element_type=F32)
        out = out + jnp.dot(inv_hi_ref[...], low, preferred_element_type=F32)
        out = out + jnp.dot(inv_lo_ref[...], high, preferred_element_type=F32)
        gated_ref[...] = (filtered[0] * out).astype(BF16)

    whole = lambda a: pl.BlockSpec(a.shape, lambda i: (0,) * a.ndim)
    operands = [rim, taps, spectrum, *forward, *inverse]
    return pl.pallas_call(
        kernel,
        grid=(steps,),
        in_specs=[pl.BlockSpec((block, width), lambda i: (i, 0))] + [whole(a) for a in operands],
        out_specs=pl.BlockSpec((block, channels), lambda i: (i, 0)),
        out_shape=jax.ShapeDtypeStruct((rows, channels), BF16),
        scratch_shapes=[
            pltpu.VMEM((16, width), F32),
            pltpu.VMEM((256, channels), BF16),
        ],
        compiler_params=PARAMS,
        cost_estimate=cost(3.5),
    )(mixed, *operands)


def out_kernel(*refs):
    pieces, (low_ref, high_ref), out_ref = refs[:9], refs[9:11], refs[-1]
    channels = low_ref.shape[2]
    opposite = jnp.where(pl.program_id(0) == 0, pieces[8][...], pieces[7][...])
    blocks = [piece[...] for piece in pieces[:7]] + [opposite]
    for side, ref in enumerate((low_ref, high_ref)):
        total = jnp.zeros((out_ref.shape[0], channels), F32)
        for k, block in zip((0, 1, 7, 2, 6, 3, 5, 4), blocks):
            weight = ref[4 * k : 4 * k + 4].reshape(-1, channels)
            total = total + jnp.dot(block, weight, preferred_element_type=F32)
        out_ref[:, side * channels : (side + 1) * channels] = total.astype(BF16)


def out_projection(pieces, gathered, previous, first_block, rows_all):
    rows, channels = pieces[0].shape
    block = rows // 2
    operands = [*pieces, in_hbm(gathered), in_hbm(gathered)]
    in_specs = (
        [pl.BlockSpec((block, channels), lambda i: (i, 0))] * 7
        + [pl.BlockSpec((block, channels), lambda i: (0, 0))] * 2
        + [
            pl.BlockSpec((32, 64, channels), lambda i: (0, 0, 0)),
            pl.BlockSpec((32, 64, channels), lambda i: (0, 1, 0)),
        ]
    )
    aliases = {}
    if previous is not None:
        aliases = {len(operands): 0}
        operands.append(previous)
        in_specs.append(pl.BlockSpec(memory_space=pl.ANY))
    return pl.pallas_call(
        out_kernel,
        grid=(2,),
        in_specs=in_specs,
        out_specs=pl.BlockSpec((block, 2 * channels), lambda i: (i + first_block, 0)),
        out_shape=jax.ShapeDtypeStruct((rows_all, 2 * channels), BF16),
        input_output_aliases=aliases,
        compiler_params=PARAMS,
        cost_estimate=cost(2.3),
    )(*operands)


def halves_kernel(ahead_ref, back_ref, ahead_out_ref, back_out_ref):
    ahead_out_ref[...] = ahead_ref[...]
    back_out_ref[...] = back_ref[...]


def halves(ahead, back):
    rows, depth = ahead.shape
    block = rows // 4
    return pl.pallas_call(
        halves_kernel,
        grid=(2,),
        in_specs=[
            pl.BlockSpec((block, depth), lambda i: (i + 2, 0)),
            pl.BlockSpec((block, depth), lambda i: (i, 0)),
        ],
        out_specs=[pl.BlockSpec((block, depth), lambda i: (i, 0))] * 2,
        out_shape=[jax.ShapeDtypeStruct((rows // 2, depth), BF16)] * 2,
        compiler_params=PARAMS,
        cost_estimate=cost(0.5),
    )(ahead, back)


def folding_kernel(rows_ref, after_ref, more_ref, out_ref):
    depth, width = rows_ref.shape
    out_ref[:depth] = rows_ref[:, : width // 2]
    out_ref[depth:] = rows_ref[:, width // 2 :]


def folded(rows, after, more):
    depth, width = rows.shape
    shape = (2 * depth, width // 2)
    return pl.pallas_call(
        folding_kernel,
        grid=(1,),
        in_specs=[
            pl.BlockSpec(rows.shape, lambda i: (0, 0)),
            pl.BlockSpec(memory_space=pl.ANY),
            pl.BlockSpec(memory_space=pl.ANY),
        ],
        out_specs=pl.BlockSpec(shape, lambda i: (0, 0)),
        out_shape=jax.ShapeDtypeStruct(shape, BF16),
        compiler_params=PARAMS,
        cost_estimate=cost(0.5),
    )(rows, in_hbm(after), in_hbm(more))


def both_ways(ahead, back):
    return moved(ahead, "tensor", 1), moved(back, "tensor", -1)


def ring(block):
    ahead = back = block
    pieces = [block]
    for _ in range(3):
        ahead, back = both_ways(ahead, back)
        pieces += [ahead, back]
    return pieces + list(both_ways(*halves(ahead, back)))


def per_device(
    tokens,
    in_weight,
    adapter_down_maps,
    adapter_up_maps,
    short_filter,
    long_filter,
    skip,
    out_weight,
    adapter_ids,
):
    tok = tokens[0]
    ids = adapter_ids.reshape(1, -1)
    rows, depth = tok.shape
    channels = in_weight.shape[2]
    rank = adapter_down_maps.shape[2]
    seq, tensor, adapter = (lax.axis_index(name) for name in ("seq", "tensor", "adapter"))
    place = tensor.astype(jnp.int32).reshape(1)
    weight = in_hbm(in_weight.transpose(1, 0, 2))
    taps = short_filter.transpose(1, 0, 2)

    half = rows // 2
    f1, b1 = both_ways(tok, tok)
    f2, b2 = both_ways(f1, b1)
    f3, b3 = both_ways(f2, b2)
    f3_half, b3_half = halves(in_hbm(f3), in_hbm(b3))
    f4, b4 = both_ways(f3_half, b3_half)

    up = adapter_up_maps[0].transpose(1, 0, 2).reshape(-1, channels)
    up_all = lax.all_gather(up, ("seq", "adapter"), axis=0)
    acc = first_acc = projecting(place, None, (tok, f1, b1), (0, 1, 7), weight)
    down_all = lax.all_to_all(
        jnp.broadcast_to(adapter_down_maps[0].T[None], (32, rank, depth)),
        ("seq", "adapter"), split_axis=0, concat_axis=0, tiled=True,
    )
    forward, of_taps, inverse = (jnp.asarray(a) for a in waves())
    spectrum = jnp.dot(
        of_taps, long_filter.at[0].add(skip), precision=lax.Precision.HIGHEST
    )
    partials = partial_codes(tok, ids, down_all.reshape(-1, depth), (acc, f2, b2))
    received = lax.all_to_all(partials, "tensor", split_axis=0, concat_axis=0, tiled=True)
    acc = projecting(place, acc, (f2, b2), (2, 6), weight)
    codes = lax.all_to_all(
        summed_codes(received, (acc, f3_half, b3_half)), "tensor", split_axis=0, concat_axis=0, tiled=True
    )

    acc = projecting(place, acc, (f3, b3), (3, 5), weight)
    quarter = out_weight.shape[0] // 4
    out_rows = lax.dynamic_slice(
        out_weight,
        (adapter * quarter, ((tensor + seq) % 8) * depth),
        (quarter, depth),
    )
    out_rows = lax.ppermute(
        folded(out_rows, first_acc, spectrum),
        ("seq", "tensor"),
        [(s * 8 + z, s * 8 + (z + s) % 8) for s in range(8) for z in range(8)],
    )
    out_all = lax.all_gather(out_rows, ("seq", "adapter"), axis=0)

    shared = (weight, codes, ids, up_all, taps)
    mixed_late, rim_late = mixing(place, acc, f4, 4, *shared, half // 256)
    rim_in = lax.ppermute(rim_late, "seq", [(i, i + 1) for i in range(7)])
    mixed_early, rim_early = mixing(place, acc, b4, 4, *shared, 0)

    filters = (taps, spectrum, split(forward), split(inverse))
    gated_early = ring(filtering(mixed_early, rim_in, *filters))
    gated_late = ring(filtering(mixed_late, rim_early, *filters))
    out = out_projection(gated_early, out_all, None, 0, rows)
    out = out_projection(gated_late, out_all, out, 2, rows)
    return out[None]


def solution(mesh):
    return jax.shard_map(
        per_device,
        mesh=mesh,
        in_specs=(
            P("adapter", "seq", "tensor"),
            P(None, None, "tensor"),
            P(("seq", "adapter"), "tensor", None),
            P(("seq", "adapter"), None, None, "tensor"),
            P(None, None, "tensor"),
            P(None, "tensor"),
            P("tensor"),
            P("tensor", None),
            P("adapter", "seq", None),
        ),
        out_specs=P("adapter", "seq", "tensor"),
        check_vma=False,
    )
```

```python
import jax
import jax.numpy as jnp
import numpy as np
from jax import lax
from jax.experimental import pallas as pl
from jax.experimental.pallas import tpu as pltpu
from jax.sharding import PartitionSpec as P

F32 = jnp.float32
BF16 = jnp.bfloat16
PARAMS = pltpu.CompilerParams(vmem_limit_bytes=24 * 1024 * 1024)


def cost(micros):
    return pl.CostEstimate(
        flops=int(micros * 2e9), transcendentals=0, bytes_accessed=int(micros * 2e6)
    )


def in_hbm(array):
    return pltpu.with_memory_space_constraint(array, pltpu.HBM)


def moved(block, axis, distance):
    n = lax.axis_size(axis)
    return lax.ppermute(block, axis, [(i, (i + distance) % n) for i in range(n)])


def nt_dot(a, b):
    return lax.dot_general(a, b, (((1,), (1,)), ((), ())), preferred_element_type=F32)


def codes_kernel(tok_ref, ids_ref, down_ref, *refs):
    out_ref = refs[-1]
    tok = tok_ref[...]
    ids = ids_ref[...]
    total = jnp.zeros((64, tok.shape[0]), F32)
    half = down_ref.shape[0] // 2
    for side in range(2):
        products = nt_dot(down_ref[side * half : (side + 1) * half], tok)
        for own in range(half // 64):
            total = total + jnp.where(
                ids == side * (half // 64) + own, products[own * 64 : own * 64 + 64], 0.0
            )
    for j in range(out_ref.shape[0]):
        out_ref[j] = total[:, 128 * j : 128 * j + 128]


def partial_codes(tok, ids, down, after):
    rows, depth = tok.shape
    block = 256
    return pl.pallas_call(
        codes_kernel,
        grid=(rows // block,),
        in_specs=[
            pl.BlockSpec((block, depth), lambda i: (i, 0)),
            pl.BlockSpec((1, block), lambda i: (0, i)),
            pl.BlockSpec(down.shape, lambda i: (0, 0)),
        ]
        + [pl.BlockSpec(memory_space=pl.ANY) for _ in after],
        out_specs=pl.BlockSpec((block // 128, 64, 128), lambda i: (i, 0, 0)),
        out_shape=jax.ShapeDtypeStruct((rows // 128, 64, 128), F32),
        compiler_params=PARAMS,
        cost_estimate=cost(4.0),
    )(in_hbm(tok), ids, down, *[in_hbm(a) for a in after])


def sum_kernel(parts_ref, *refs):
    out_ref = refs[-1]
    total = parts_ref[0]
    for j in range(1, parts_ref.shape[0]):
        total = total + parts_ref[j]
    total = total.astype(BF16)
    for j in range(out_ref.shape[0]):
        out_ref[j] = total


def summed_codes(parts, after):
    whole = pl.BlockSpec(parts.shape, lambda i: (0, 0, 0))
    return pl.pallas_call(
        sum_kernel,
        grid=(1,),
        in_specs=[whole] + [pl.BlockSpec(memory_space=pl.ANY) for _ in after],
        out_specs=whole,
        out_shape=jax.ShapeDtypeStruct(parts.shape, BF16),
        compiler_params=PARAMS,
        cost_estimate=cost(0.5),
    )(parts, *[in_hbm(a) for a in after])


def weight_spec(weight, k):
    parts, depth, channels = weight.shape
    return pl.BlockSpec(
        (parts, depth // 8, channels), lambda i, place: (0, (place[0] + 8 - k) % 8, 0)
    )


def projecting(place, acc, pieces, ks, weight):
    rows, depth = pieces[0].shape
    block = 256
    parts, _, channels = weight.shape
    width = parts * channels
    old = [] if acc is None else [in_hbm(acc)]
    n = len(pieces)

    def kernel(place_ref, *refs):
        total_in, refs = refs[: len(old)], refs[len(old) :]
        weights, out_ref = refs[n : 2 * n], refs[-1]
        loaded = [piece[...] for piece in refs[:n]]
        for c in range(parts):
            lanes = slice(c * channels, (c + 1) * channels)
            total = jnp.dot(loaded[0], weights[0][c], preferred_element_type=F32)
            for piece, ref in zip(loaded[1:], weights[1:]):
                total = total + jnp.dot(piece, ref[c], preferred_element_type=F32)
            if old:
                total = total + total_in[0][:, lanes]
            out_ref[:, lanes] = total

    acc_spec = pl.BlockSpec((block, width), lambda i, place: (i, 0))
    return pl.pallas_call(
        kernel,
        grid_spec=pltpu.PrefetchScalarGridSpec(
            num_scalar_prefetch=1,
            grid=(rows // block,),
            in_specs=[acc_spec for _ in old]
            + [pl.BlockSpec((block, depth), lambda i, place: (i, 0)) for _ in pieces]
            + [weight_spec(weight, k) for k in ks],
            out_specs=acc_spec,
        ),
        out_shape=jax.ShapeDtypeStruct((rows, width), F32),
        compiler_params=PARAMS,
        cost_estimate=cost(0.0045 * rows),
    )(place, *old, *[in_hbm(piece) for piece in pieces], *[weight for _ in ks])


def mixing(place, acc, last, k, weight, codes, ids, gathered, taps, first_block):
    rows, width = last.shape[0], acc.shape[1]
    block = 256
    steps = rows // block
    depth = last.shape[1]
    channels = width // 3

    def kernel(
        place_ref, acc_ref, last_ref, weight_ref, codes_ref, ids_ref,
        u0_ref, u1_ref, u2_ref, taps_ref, mixed_ref, rim_ref,
    ):
        step = pl.program_id(0)
        packed = codes_ref[...].astype(F32)
        low = jnp.concatenate([packed[j].T for j in range(2)], axis=0).astype(BF16)
        low = jnp.concatenate([low, low], axis=1)
        upper = (lax.broadcasted_iota(jnp.int32, (1, 128), 1) // 64).astype(F32)
        ids_block = jnp.broadcast_to(ids_ref[...].astype(F32), (128, block)).T
        zero = jnp.zeros_like(low)
        spread = jnp.concatenate(
            [jnp.where(ids_block == upper + 2.0 * pair, low, zero) for pair in range(16)], axis=1
        )
        for c, ref in enumerate((u0_ref, u1_ref, u2_ref)):
            lanes = slice(c * channels, (c + 1) * channels)
            total = acc_ref[:, lanes]
            total = total + jnp.dot(last_ref[...], weight_ref[c], preferred_element_type=F32)
            up = ref[...].reshape(-1, channels)
            delta = jnp.dot(spread, up, preferred_element_type=F32).astype(BF16)
            mixed_ref[:, lanes] = (total + delta.astype(F32)).astype(BF16)

        @pl.when(step == steps - 1)
        def _():
            branches = []
            for c in (1, 2):
                lanes = slice(c * channels, (c + 1) * channels)
                tail = mixed_ref[:, lanes].astype(F32)
                running = jnp.zeros((128, channels), F32)
                for tap in range(7):
                    running = (
                        running
                        + taps_ref[c, tap : tap + 1, :] * tail[block - 128 - tap : block - tap]
                    )
                branches.append(running)
            rim_ref[:128] = (branches[0] * branches[1]).astype(BF16)
            for c in range(3):
                rim_ref[128 + 16 * c : 144 + 16 * c] = mixed_ref[
                    block - 16 :, c * channels : (c + 1) * channels
                ]

    def up_spec(c):
        return pl.BlockSpec((32, 64, channels), lambda i, place: (0, c, 0))

    return pl.pallas_call(
        kernel,
        grid_spec=pltpu.PrefetchScalarGridSpec(
            num_scalar_prefetch=1,
            grid=(steps,),
            in_specs=[
                pl.BlockSpec((block, width), lambda i, place: (i + first_block, 0)),
                pl.BlockSpec((block, depth), lambda i, place: (i, 0)),
                weight_spec(weight, k),
                pl.BlockSpec((2, 64, 128), lambda i, place: (i + first_block, 0, 0)),
                pl.BlockSpec((1, block), lambda i, place: (0, i + first_block)),
                up_spec(0),
                up_spec(1),
                up_spec(2),
                pl.BlockSpec(taps.shape, lambda i, place: (0, 0, 0)),
            ],
            out_specs=[
                pl.BlockSpec((block, width), lambda i, place: (i, 0)),
                pl.BlockSpec((176, channels), lambda i, place: (0, 0)),
            ],
        ),
        out_shape=[
            jax.ShapeDtypeStruct((rows, width), BF16),
            jax.ShapeDtypeStruct((176, channels), BF16),
        ],
        compiler_params=PARAMS,
        cost_estimate=cost(4.0),
    )(place, in_hbm(acc), last, weight, codes, ids, *[in_hbm(gathered)] * 3, taps)


def split(array):
    high = array.astype(BF16)
    return high, (array - high.astype(F32)).astype(BF16)


def waves():
    size = 256
    half = size // 2
    k, t = np.arange(half)[:, None], np.arange(size)[None, :]
    angle = 2.0 * np.pi * ((k * t) % size) / size
    cosine, sine = np.cos(angle), np.sin(angle)
    alternating = 1.0 - 2.0 * (np.arange(size) % 2)
    nyquist_first = sine.copy()
    nyquist_first[0] = -alternating
    forward = np.concatenate([cosine, -nyquist_first], 0)
    last = cosine.copy()
    last[0] = alternating
    of_taps = np.concatenate([cosine, -sine, last], 0)[:, :half]
    weights = np.full((half, 1), 2.0 / size)
    weights[0] = 1.0 / size
    inverse = np.concatenate([cosine * weights, -nyquist_first * weights], 0).T[half:]
    return [np.asarray(a, np.float32) for a in (forward, of_taps, inverse)]


def filtering(mixed, rim, taps, spectrum, forward, inverse):
    block = 256
    rows, width = mixed.shape
    channels = width // 3
    steps = rows // block

    def kernel(
        mixed_ref, rim_ref, taps_ref, spectrum_ref, fwd_hi_ref, fwd_lo_ref, inv_hi_ref, inv_lo_ref,
        gated_ref, before_ref, window_ref,
    ):
        step = pl.program_id(0)
        current = mixed_ref[...].astype(F32)

        @pl.when(step == 0)
        def _():
            window_ref[:128] = rim_ref[:128]
            for c in range(3):
                before_ref[:, c * channels : (c + 1) * channels] = rim_ref[
                    128 + 16 * c : 144 + 16 * c
                ].astype(F32)

        @pl.when(step > 0)
        def _():
            window_ref[:128] = window_ref[block:]

        filtered = []
        for c in range(3):
            lanes = slice(c * channels, (c + 1) * channels)
            extended = jnp.concatenate([before_ref[:, lanes], current[:, lanes]], axis=0)
            running = jnp.zeros((block, channels), F32)
            for tap in range(7):
                running = running + taps_ref[c, tap : tap + 1, :] * extended[16 - tap : 16 - tap + block]
            filtered.append(running)
        before_ref[...] = current[block - 16 :]
        window_ref[128:] = (filtered[1] * filtered[2]).astype(BF16)
        first, second, third = (spectrum_ref[128 * j : 128 * j + 128] for j in range(3))
        for start in range(0, block, 128):
            window = window_ref[start : start + 256]
            waves_in = jnp.dot(fwd_hi_ref[...], window, preferred_element_type=F32)
            waves_in = waves_in + jnp.dot(fwd_lo_ref[...], window, preferred_element_type=F32)
            real, imaginary = waves_in[:128], waves_in[128:]
            product = jnp.concatenate(
                [real * first - imaginary * second, real * second + imaginary * third], axis=0
            )
            high, low = split(product)
            out = jnp.dot(inv_hi_ref[...], high, preferred_element_type=F32)
            out = out + jnp.dot(inv_hi_ref[...], low, preferred_element_type=F32)
            out = out + jnp.dot(inv_lo_ref[...], high, preferred_element_type=F32)
            query = filtered[0][start : start + 128]
            gated_ref[start : start + 128] = (query * out).astype(BF16)

    whole = lambda a: pl.BlockSpec(a.shape, lambda i: (0,) * a.ndim)
    operands = [rim, taps, spectrum, *forward, *inverse]
    return pl.pallas_call(
        kernel,
        grid=(steps,),
        in_specs=[pl.BlockSpec((block, width), lambda i: (i, 0))] + [whole(a) for a in operands],
        out_specs=pl.BlockSpec((block, channels), lambda i: (i, 0)),
        out_shape=jax.ShapeDtypeStruct((rows, channels), BF16),
        scratch_shapes=[
            pltpu.VMEM((16, width), F32),
            pltpu.VMEM((128 + block, channels), BF16),
        ],
        compiler_params=PARAMS,
        cost_estimate=cost(3.5),
    )(mixed, *operands)


def out_kernel(*refs):
    pieces, (low_ref, high_ref), out_ref = refs[:9], refs[9:11], refs[-1]
    channels = low_ref.shape[2]
    opposite = jnp.where(pl.program_id(0) == 0, pieces[8][...], pieces[7][...])
    blocks = [piece[...] for piece in pieces[:7]] + [opposite]
    for side, ref in enumerate((low_ref, high_ref)):
        total = jnp.zeros((out_ref.shape[0], channels), F32)
        for k, block in zip((0, 1, 7, 2, 6, 3, 5, 4), blocks):
            weight = ref[4 * k : 4 * k + 4].reshape(-1, channels)
            total = total + jnp.dot(block, weight, preferred_element_type=F32)
        out_ref[:, side * channels : (side + 1) * channels] = total.astype(BF16)


def out_projection(pieces, gathered, previous, first_block, rows_all):
    rows, channels = pieces[0].shape
    block = rows // 2
    operands = [*pieces, in_hbm(gathered), in_hbm(gathered)]
    in_specs = (
        [pl.BlockSpec((block, channels), lambda i: (i, 0))] * 7
        + [pl.BlockSpec((block, channels), lambda i: (0, 0))] * 2
        + [
            pl.BlockSpec((32, 64, channels), lambda i: (0, 0, 0)),
            pl.BlockSpec((32, 64, channels), lambda i: (0, 1, 0)),
        ]
    )
    aliases = {}
    if previous is not None:
        aliases = {len(operands): 0}
        operands.append(previous)
        in_specs.append(pl.BlockSpec(memory_space=pl.ANY))
    return pl.pallas_call(
        out_kernel,
        grid=(2,),
        in_specs=in_specs,
        out_specs=pl.BlockSpec((block, 2 * channels), lambda i: (i + first_block, 0)),
        out_shape=jax.ShapeDtypeStruct((rows_all, 2 * channels), BF16),
        input_output_aliases=aliases,
        compiler_params=PARAMS,
        cost_estimate=cost(2.3),
    )(*operands)


def halves_kernel(ahead_ref, back_ref, ahead_out_ref, back_out_ref):
    ahead_out_ref[...] = ahead_ref[...]
    back_out_ref[...] = back_ref[...]


def halves(ahead, back):
    rows, depth = ahead.shape
    block = rows // 4
    return pl.pallas_call(
        halves_kernel,
        grid=(2,),
        in_specs=[
            pl.BlockSpec((block, depth), lambda i: (i + 2, 0)),
            pl.BlockSpec((block, depth), lambda i: (i, 0)),
        ],
        out_specs=[pl.BlockSpec((block, depth), lambda i: (i, 0))] * 2,
        out_shape=[jax.ShapeDtypeStruct((rows // 2, depth), BF16)] * 2,
        compiler_params=PARAMS,
        cost_estimate=cost(0.5),
    )(ahead, back)


def folding_kernel(rows_ref, after_ref, more_ref, out_ref):
    depth, width = rows_ref.shape
    out_ref[:depth] = rows_ref[:, : width // 2]
    out_ref[depth:] = rows_ref[:, width // 2 :]


def folded(rows, after, more):
    depth, width = rows.shape
    shape = (2 * depth, width // 2)
    return pl.pallas_call(
        folding_kernel,
        grid=(1,),
        in_specs=[
            pl.BlockSpec(rows.shape, lambda i: (0, 0)),
            pl.BlockSpec(memory_space=pl.ANY),
            pl.BlockSpec(memory_space=pl.ANY),
        ],
        out_specs=pl.BlockSpec(shape, lambda i: (0, 0)),
        out_shape=jax.ShapeDtypeStruct(shape, BF16),
        compiler_params=PARAMS,
        cost_estimate=cost(0.5),
    )(rows, in_hbm(after), in_hbm(more))


def both_ways(ahead, back):
    return moved(ahead, "tensor", 1), moved(back, "tensor", -1)


def ring(block):
    ahead = back = block
    pieces = [block]
    for _ in range(3):
        ahead, back = both_ways(ahead, back)
        pieces += [ahead, back]
    return pieces + list(both_ways(*halves(ahead, back)))


def per_device(
    tokens,
    in_weight,
    adapter_down_maps,
    adapter_up_maps,
    short_filter,
    long_filter,
    skip,
    out_weight,
    adapter_ids,
):
    tok = tokens[0]
    ids = adapter_ids.reshape(1, -1)
    rows, depth = tok.shape
    channels = in_weight.shape[2]
    rank = adapter_down_maps.shape[2]
    seq, tensor, adapter = (lax.axis_index(name) for name in ("seq", "tensor", "adapter"))
    place = tensor.astype(jnp.int32).reshape(1)
    weight = in_hbm(in_weight.transpose(1, 0, 2))
    taps = short_filter.transpose(1, 0, 2)

    half = rows // 2
    f1, b1 = both_ways(tok, tok)
    f2, b2 = both_ways(f1, b1)
    f3, b3 = both_ways(f2, b2)
    f3_half, b3_half = halves(in_hbm(f3), in_hbm(b3))
    f4, b4 = both_ways(f3_half, b3_half)

    up = adapter_up_maps[0].transpose(1, 0, 2).reshape(-1, channels)
    up_all = lax.all_gather(up, ("seq", "adapter"), axis=0)
    acc = first_acc = projecting(place, None, (tok, f1, b1), (0, 1, 7), weight)
    down_all = lax.all_to_all(
        jnp.broadcast_to(adapter_down_maps[0].T[None], (32, rank, depth)),
        ("seq", "adapter"), split_axis=0, concat_axis=0, tiled=True,
    )
    forward, of_taps, inverse = (jnp.asarray(a) for a in waves())
    spectrum = jnp.dot(of_taps, long_filter, precision=lax.Precision.HIGHEST)
    spectrum = spectrum + of_taps[:, :1] * skip[None]
    partials = partial_codes(tok, ids, down_all.reshape(-1, depth), (acc, f2, b2))
    received = lax.all_to_all(partials, "tensor", split_axis=0, concat_axis=0, tiled=True)
    acc = projecting(place, acc, (f2, b2), (2, 6), weight)
    codes = lax.all_to_all(
        summed_codes(received, (acc, f3_half, b3_half)), "tensor", split_axis=0, concat_axis=0, tiled=True
    )

    acc = projecting(place, acc, (f3, b3), (3, 5), weight)
    quarter = out_weight.shape[0] // 4
    out_rows = lax.dynamic_slice(
        out_weight,
        (adapter * quarter, ((tensor + seq) % 8) * depth),
        (quarter, depth),
    )
    out_rows = lax.ppermute(
        folded(out_rows, first_acc, spectrum),
        ("seq", "tensor"),
        [(s * 8 + z, s * 8 + (z + s) % 8) for s in range(8) for z in range(8)],
    )
    out_all = lax.all_gather(out_rows, ("seq", "adapter"), axis=0)

    shared = (weight, codes, ids, up_all, taps)
    mixed_late, rim_late = mixing(place, acc, f4, 4, *shared, half // 256)
    rim_in = lax.ppermute(rim_late, "seq", [(i, i + 1) for i in range(7)])
    mixed_early, rim_early = mixing(place, acc, b4, 4, *shared, 0)

    filters = (taps, spectrum, split(forward), split(inverse))
    gated_early = ring(filtering(mixed_early, rim_in, *filters))
    gated_late = ring(filtering(mixed_late, rim_early, *filters))
    out = out_projection(gated_early, out_all, None, 0, rows)
    out = out_projection(gated_late, out_all, out, 2, rows)
    return out[None]


def solution(mesh):
    return jax.shard_map(
        per_device,
        mesh=mesh,
        in_specs=(
            P("adapter", "seq", "tensor"),
            P(None, None, "tensor"),
            P(("seq", "adapter"), "tensor", None),
            P(("seq", "adapter"), None, None, "tensor"),
            P(None, None, "tensor"),
            P(None, "tensor"),
            P("tensor"),
            P("tensor", None),
            P("adapter", "seq", None),
        ),
        out_specs=P("adapter", "seq", "tensor"),
        check_vma=False,
    )
```

```python
import jax
import jax.numpy as jnp
import numpy as np
from jax import lax
from jax.experimental import pallas as pl
from jax.experimental.pallas import tpu as pltpu
from jax.sharding import PartitionSpec as P

F32 = jnp.float32
BF16 = jnp.bfloat16
PARAMS = pltpu.CompilerParams(vmem_limit_bytes=24 * 1024 * 1024)


def cost(micros):
    return pl.CostEstimate(
        flops=int(micros * 2.4e9), transcendentals=0, bytes_accessed=int(micros * 2.4e6)
    )


def in_hbm(array):
    return pltpu.with_memory_space_constraint(array, pltpu.HBM)


def moved(block, axis, distance):
    n = lax.axis_size(axis)
    return lax.ppermute(block, axis, [(i, (i + distance) % n) for i in range(n)])


def nt_dot(a, b):
    return lax.dot_general(a, b, (((1,), (1,)), ((), ())), preferred_element_type=F32)


def codes_kernel(tok_ref, ids_ref, down_ref, *refs):
    out_ref = refs[-1]
    tok = tok_ref[...]
    ids = ids_ref[...]
    total = jnp.zeros((64, tok.shape[0]), F32)
    half = down_ref.shape[0] // 2
    for side in range(2):
        products = nt_dot(down_ref[side * half : (side + 1) * half], tok)
        for own in range(half // 64):
            total = total + jnp.where(
                ids == side * (half // 64) + own, products[own * 64 : own * 64 + 64], 0.0
            )
    for j in range(out_ref.shape[0]):
        out_ref[j] = total[:, 128 * j : 128 * j + 128]


def partial_codes(tok, ids, down, after):
    rows, depth = tok.shape
    block = 256
    return pl.pallas_call(
        codes_kernel,
        grid=(rows // block,),
        in_specs=[
            pl.BlockSpec((block, depth), lambda i: (i, 0)),
            pl.BlockSpec((1, block), lambda i: (0, i)),
            pl.BlockSpec(down.shape, lambda i: (0, 0)),
        ]
        + [pl.BlockSpec(memory_space=pl.ANY) for _ in after],
        out_specs=pl.BlockSpec((block // 128, 64, 128), lambda i: (i, 0, 0)),
        out_shape=jax.ShapeDtypeStruct((rows // 128, 64, 128), F32),
        compiler_params=PARAMS,
        cost_estimate=cost(4.0),
    )(in_hbm(tok), ids, down, *[in_hbm(a) for a in after])


def sum_kernel(parts_ref, *refs):
    out_ref = refs[-1]
    total = parts_ref[0]
    for j in range(1, parts_ref.shape[0]):
        total = total + parts_ref[j]
    total = total.astype(BF16)
    for j in range(out_ref.shape[0]):
        out_ref[j] = total


def summed_codes(parts, after):
    whole = pl.BlockSpec(parts.shape, lambda i: (0, 0, 0))
    return pl.pallas_call(
        sum_kernel,
        grid=(1,),
        in_specs=[whole] + [pl.BlockSpec(memory_space=pl.ANY) for _ in after],
        out_specs=whole,
        out_shape=jax.ShapeDtypeStruct(parts.shape, BF16),
        compiler_params=PARAMS,
        cost_estimate=cost(0.5),
    )(parts, *[in_hbm(a) for a in after])


def weight_spec(weight, k):
    parts, depth, channels = weight.shape
    return pl.BlockSpec(
        (parts, depth // 8, channels), lambda i, place: (0, (place[0] + 8 - k) % 8, 0)
    )


def projecting(place, acc, pieces, ks, weight):
    rows, depth = pieces[0].shape
    block = 256
    parts, _, channels = weight.shape
    width = parts * channels
    old = [] if acc is None else [in_hbm(acc)]
    n = len(pieces)

    def kernel(place_ref, *refs):
        total_in, refs = refs[: len(old)], refs[len(old) :]
        weights, out_ref = refs[n : 2 * n], refs[-1]
        loaded = [piece[...] for piece in refs[:n]]
        for c in range(parts):
            lanes = slice(c * channels, (c + 1) * channels)
            total = jnp.dot(loaded[0], weights[0][c], preferred_element_type=F32)
            for piece, ref in zip(loaded[1:], weights[1:]):
                total = total + jnp.dot(piece, ref[c], preferred_element_type=F32)
            if old:
                total = total + total_in[0][:, lanes]
            out_ref[:, lanes] = total

    acc_spec = pl.BlockSpec((block, width), lambda i, place: (i, 0))
    return pl.pallas_call(
        kernel,
        grid_spec=pltpu.PrefetchScalarGridSpec(
            num_scalar_prefetch=1,
            grid=(rows // block,),
            in_specs=[acc_spec for _ in old]
            + [pl.BlockSpec((block, depth), lambda i, place: (i, 0)) for _ in pieces]
            + [weight_spec(weight, k) for k in ks],
            out_specs=acc_spec,
        ),
        out_shape=jax.ShapeDtypeStruct((rows, width), F32),
        compiler_params=PARAMS,
        cost_estimate=cost(0.0045 * rows),
    )(place, *old, *[in_hbm(piece) for piece in pieces], *[weight for _ in ks])


def mixing(place, acc, last, k, weight, codes, ids, gathered, taps, first_block):
    rows, width = last.shape[0], acc.shape[1]
    block = 256
    steps = rows // block
    depth = last.shape[1]
    channels = width // 3

    def kernel(
        place_ref, acc_ref, last_ref, weight_ref, codes_ref, ids_ref,
        u0_ref, u1_ref, u2_ref, taps_ref, mixed_ref, rim_ref,
    ):
        step = pl.program_id(0)
        packed = codes_ref[...].astype(F32)
        low = jnp.concatenate([packed[j].T for j in range(2)], axis=0).astype(BF16)
        low = jnp.concatenate([low, low], axis=1)
        upper = (lax.broadcasted_iota(jnp.int32, (1, 128), 1) // 64).astype(F32)
        ids_block = jnp.broadcast_to(ids_ref[...].astype(F32), (128, block)).T
        zero = jnp.zeros_like(low)
        spread = jnp.concatenate(
            [jnp.where(ids_block == upper + 2.0 * pair, low, zero) for pair in range(16)], axis=1
        )
        for c, ref in enumerate((u0_ref, u1_ref, u2_ref)):
            lanes = slice(c * channels, (c + 1) * channels)
            total = acc_ref[:, lanes]
            total = total + jnp.dot(last_ref[...], weight_ref[c], preferred_element_type=F32)
            up = ref[...].reshape(-1, channels)
            delta = jnp.dot(spread, up, preferred_element_type=F32).astype(BF16)
            mixed_ref[:, lanes] = (total + delta.astype(F32)).astype(BF16)

        @pl.when(step == steps - 1)
        def _():
            branches = []
            for c in (1, 2):
                lanes = slice(c * channels, (c + 1) * channels)
                tail = mixed_ref[:, lanes].astype(F32)
                running = jnp.zeros((128, channels), F32)
                for tap in range(7):
                    running = (
                        running
                        + taps_ref[c, tap : tap + 1, :] * tail[block - 128 - tap : block - tap]
                    )
                branches.append(running)
            rim_ref[:128] = (branches[0] * branches[1]).astype(BF16)
            for c in range(3):
                rim_ref[128 + 16 * c : 144 + 16 * c] = mixed_ref[
                    block - 16 :, c * channels : (c + 1) * channels
                ]

    def up_spec(c):
        return pl.BlockSpec((32, 64, channels), lambda i, place: (0, c, 0))

    return pl.pallas_call(
        kernel,
        grid_spec=pltpu.PrefetchScalarGridSpec(
            num_scalar_prefetch=1,
            grid=(steps,),
            in_specs=[
                pl.BlockSpec((block, width), lambda i, place: (i + first_block, 0)),
                pl.BlockSpec((block, depth), lambda i, place: (i, 0)),
                weight_spec(weight, k),
                pl.BlockSpec((2, 64, 128), lambda i, place: (i + first_block, 0, 0)),
                pl.BlockSpec((1, block), lambda i, place: (0, i + first_block)),
                up_spec(0),
                up_spec(1),
                up_spec(2),
                pl.BlockSpec(taps.shape, lambda i, place: (0, 0, 0)),
            ],
            out_specs=[
                pl.BlockSpec((block, width), lambda i, place: (i, 0)),
                pl.BlockSpec((176, channels), lambda i, place: (0, 0)),
            ],
        ),
        out_shape=[
            jax.ShapeDtypeStruct((rows, width), BF16),
            jax.ShapeDtypeStruct((176, channels), BF16),
        ],
        compiler_params=PARAMS,
        cost_estimate=cost(4.0),
    )(place, in_hbm(acc), last, weight, codes, ids, *[in_hbm(gathered)] * 3, taps)


def split(array):
    high = array.astype(BF16)
    return high, (array - high.astype(F32)).astype(BF16)


def waves():
    size = 256
    half = size // 2
    k, t = np.arange(half)[:, None], np.arange(size)[None, :]
    angle = 2.0 * np.pi * ((k * t) % size) / size
    cosine, sine = np.cos(angle), np.sin(angle)
    alternating = 1.0 - 2.0 * (np.arange(size) % 2)
    nyquist_first = sine.copy()
    nyquist_first[0] = -alternating
    forward = np.concatenate([cosine, -nyquist_first], 0)
    last = cosine.copy()
    last[0] = alternating
    of_taps = np.concatenate([cosine, -sine, last], 0)[:, :half]
    weights = np.full((half, 1), 2.0 / size)
    weights[0] = 1.0 / size
    inverse = np.concatenate([cosine * weights, -nyquist_first * weights], 0).T[half:]
    return [np.asarray(a, np.float32) for a in (forward, of_taps, inverse)]


def filtering(mixed, rim, taps, spectrum, forward, inverse):
    block = 256
    rows, width = mixed.shape
    channels = width // 3
    steps = rows // block

    def kernel(
        mixed_ref, rim_ref, taps_ref, spectrum_ref, fwd_hi_ref, fwd_lo_ref, inv_hi_ref, inv_lo_ref,
        gated_ref, before_ref, window_ref,
    ):
        step = pl.program_id(0)
        current = mixed_ref[...].astype(F32)

        @pl.when(step == 0)
        def _():
            window_ref[:128] = rim_ref[:128]
            for c in range(3):
                before_ref[:, c * channels : (c + 1) * channels] = rim_ref[
                    128 + 16 * c : 144 + 16 * c
                ].astype(F32)

        @pl.when(step > 0)
        def _():
            window_ref[:128] = window_ref[block:]

        filtered = []
        for c in range(3):
            lanes = slice(c * channels, (c + 1) * channels)
            extended = jnp.concatenate([before_ref[:, lanes], current[:, lanes]], axis=0)
            running = jnp.zeros((block, channels), F32)
            for tap in range(7):
                running = running + taps_ref[c, tap : tap + 1, :] * extended[16 - tap : 16 - tap + block]
            filtered.append(running)
        before_ref[...] = current[block - 16 :]
        window_ref[128:] = (filtered[1] * filtered[2]).astype(BF16)
        first, second, third = (spectrum_ref[128 * j : 128 * j + 128] for j in range(3))
        for start in range(0, block, 128):
            window = window_ref[start : start + 256]
            waves_in = jnp.dot(fwd_hi_ref[...], window, preferred_element_type=F32)
            waves_in = waves_in + jnp.dot(fwd_lo_ref[...], window, preferred_element_type=F32)
            real, imaginary = waves_in[:128], waves_in[128:]
            product = jnp.concatenate(
                [real * first - imaginary * second, real * second + imaginary * third], axis=0
            )
            high, low = split(product)
            out = jnp.dot(inv_hi_ref[...], high, preferred_element_type=F32)
            out = out + jnp.dot(inv_hi_ref[...], low, preferred_element_type=F32)
            out = out + jnp.dot(inv_lo_ref[...], high, preferred_element_type=F32)
            query = filtered[0][start : start + 128]
            gated_ref[start : start + 128] = (query * out).astype(BF16)

    whole = lambda a: pl.BlockSpec(a.shape, lambda i: (0,) * a.ndim)
    operands = [rim, taps, spectrum, *forward, *inverse]
    return pl.pallas_call(
        kernel,
        grid=(steps,),
        in_specs=[pl.BlockSpec((block, width), lambda i: (i, 0))] + [whole(a) for a in operands],
        out_specs=pl.BlockSpec((block, channels), lambda i: (i, 0)),
        out_shape=jax.ShapeDtypeStruct((rows, channels), BF16),
        scratch_shapes=[
            pltpu.VMEM((16, width), F32),
            pltpu.VMEM((128 + block, channels), BF16),
        ],
        compiler_params=PARAMS,
        cost_estimate=cost(3.5),
    )(mixed, *operands)


def out_kernel(*refs):
    pieces, (low_ref, high_ref), out_ref = refs[:9], refs[9:11], refs[-1]
    channels = low_ref.shape[2]
    opposite = jnp.where(pl.program_id(0) == 0, pieces[8][...], pieces[7][...])
    blocks = [piece[...] for piece in pieces[:7]] + [opposite]
    for side, ref in enumerate((low_ref, high_ref)):
        total = jnp.zeros((out_ref.shape[0], channels), F32)
        for k, block in zip((0, 1, 7, 2, 6, 3, 5, 4), blocks):
            weight = ref[4 * k : 4 * k + 4].reshape(-1, channels)
            total = total + jnp.dot(block, weight, preferred_element_type=F32)
        out_ref[:, side * channels : (side + 1) * channels] = total.astype(BF16)


def out_projection(pieces, gathered, previous, first_block, rows_all):
    rows, channels = pieces[0].shape
    block = rows // 2
    operands = [*pieces, in_hbm(gathered), in_hbm(gathered)]
    in_specs = (
        [pl.BlockSpec((block, channels), lambda i: (i, 0))] * 7
        + [pl.BlockSpec((block, channels), lambda i: (0, 0))] * 2
        + [
            pl.BlockSpec((32, 64, channels), lambda i: (0, 0, 0)),
            pl.BlockSpec((32, 64, channels), lambda i: (0, 1, 0)),
        ]
    )
    aliases = {}
    if previous is not None:
        aliases = {len(operands): 0}
        operands.append(previous)
        in_specs.append(pl.BlockSpec(memory_space=pl.ANY))
    return pl.pallas_call(
        out_kernel,
        grid=(2,),
        in_specs=in_specs,
        out_specs=pl.BlockSpec((block, 2 * channels), lambda i: (i + first_block, 0)),
        out_shape=jax.ShapeDtypeStruct((rows_all, 2 * channels), BF16),
        input_output_aliases=aliases,
        compiler_params=PARAMS,
        cost_estimate=cost(2.3),
    )(*operands)


def halves_kernel(ahead_ref, back_ref, ahead_out_ref, back_out_ref):
    ahead_out_ref[...] = ahead_ref[...]
    back_out_ref[...] = back_ref[...]


def halves(ahead, back):
    rows, depth = ahead.shape
    block = rows // 4
    return pl.pallas_call(
        halves_kernel,
        grid=(2,),
        in_specs=[
            pl.BlockSpec((block, depth), lambda i: (i + 2, 0)),
            pl.BlockSpec((block, depth), lambda i: (i, 0)),
        ],
        out_specs=[pl.BlockSpec((block, depth), lambda i: (i, 0))] * 2,
        out_shape=[jax.ShapeDtypeStruct((rows // 2, depth), BF16)] * 2,
        compiler_params=PARAMS,
        cost_estimate=cost(0.5),
    )(ahead, back)


def folding_kernel(rows_ref, after_ref, more_ref, out_ref):
    depth, width = rows_ref.shape
    out_ref[:depth] = rows_ref[:, : width // 2]
    out_ref[depth:] = rows_ref[:, width // 2 :]


def folded(rows, after, more):
    depth, width = rows.shape
    shape = (2 * depth, width // 2)
    return pl.pallas_call(
        folding_kernel,
        grid=(1,),
        in_specs=[
            pl.BlockSpec(rows.shape, lambda i: (0, 0)),
            pl.BlockSpec(memory_space=pl.ANY),
            pl.BlockSpec(memory_space=pl.ANY),
        ],
        out_specs=pl.BlockSpec(shape, lambda i: (0, 0)),
        out_shape=jax.ShapeDtypeStruct(shape, BF16),
        compiler_params=PARAMS,
        cost_estimate=cost(0.5),
    )(rows, in_hbm(after), in_hbm(more))


def both_ways(ahead, back):
    return moved(ahead, "tensor", 1), moved(back, "tensor", -1)


def ring(block):
    ahead = back = block
    pieces = [block]
    for _ in range(3):
        ahead, back = both_ways(ahead, back)
        pieces += [ahead, back]
    return pieces + list(both_ways(*halves(ahead, back)))


def per_device(
    tokens,
    in_weight,
    adapter_down_maps,
    adapter_up_maps,
    short_filter,
    long_filter,
    skip,
    out_weight,
    adapter_ids,
):
    tok = tokens[0]
    ids = adapter_ids.reshape(1, -1)
    rows, depth = tok.shape
    channels = in_weight.shape[2]
    rank = adapter_down_maps.shape[2]
    seq, tensor, adapter = (lax.axis_index(name) for name in ("seq", "tensor", "adapter"))
    place = tensor.astype(jnp.int32).reshape(1)
    weight = in_hbm(in_weight.transpose(1, 0, 2))
    taps = short_filter.transpose(1, 0, 2)

    half = rows // 2
    f1, b1 = both_ways(tok, tok)
    f2, b2 = both_ways(f1, b1)
    f3, b3 = both_ways(f2, b2)
    f3_half, b3_half = halves(in_hbm(f3), in_hbm(b3))
    f4, b4 = both_ways(f3_half, b3_half)

    up = adapter_up_maps[0].transpose(1, 0, 2).reshape(-1, channels)
    up_all = lax.all_gather(up, ("seq", "adapter"), axis=0)
    acc = first_acc = projecting(place, None, (tok, f1, b1), (0, 1, 7), weight)
    down_all = lax.all_to_all(
        jnp.broadcast_to(adapter_down_maps[0].T[None], (32, rank, depth)),
        ("seq", "adapter"), split_axis=0, concat_axis=0, tiled=True,
    )
    forward, of_taps, inverse = (jnp.asarray(a) for a in waves())
    spectrum = jnp.dot(of_taps, long_filter, precision=lax.Precision.HIGHEST)
    spectrum = spectrum + of_taps[:, :1] * skip[None]
    partials = partial_codes(tok, ids, down_all.reshape(-1, depth), (acc,))
    received = lax.all_to_all(partials, "tensor", split_axis=0, concat_axis=0, tiled=True)
    acc = projecting(place, acc, (f2, b2), (2, 6), weight)
    codes = lax.all_to_all(
        summed_codes(received, (acc,)), "tensor", split_axis=0, concat_axis=0, tiled=True
    )

    acc = projecting(place, acc, (f3, b3), (3, 5), weight)
    quarter = out_weight.shape[0] // 4
    out_rows = lax.dynamic_slice(
        out_weight,
        (adapter * quarter, ((tensor + seq) % 8) * depth),
        (quarter, depth),
    )
    out_rows = lax.ppermute(
        folded(out_rows, first_acc, spectrum),
        ("seq", "tensor"),
        [(s * 8 + z, s * 8 + (z + s) % 8) for s in range(8) for z in range(8)],
    )
    out_all = lax.all_gather(out_rows, ("seq", "adapter"), axis=0)

    shared = (weight, codes, ids, up_all, taps)
    mixed_late, rim_late = mixing(place, acc, f4, 4, *shared, half // 256)
    rim_in = lax.ppermute(rim_late, "seq", [(i, i + 1) for i in range(7)])
    mixed_early, rim_early = mixing(place, acc, b4, 4, *shared, 0)

    filters = (taps, spectrum, split(forward), split(inverse))
    gated_early = ring(filtering(mixed_early, rim_in, *filters))
    gated_late = ring(filtering(mixed_late, rim_early, *filters))
    out = out_projection(gated_early, out_all, None, 0, rows)
    out = out_projection(gated_late, out_all, out, 2, rows)
    return out[None]


def solution(mesh):
    return jax.shard_map(
        per_device,
        mesh=mesh,
        in_specs=(
            P("adapter", "seq", "tensor"),
            P(None, None, "tensor"),
            P(("seq", "adapter"), "tensor", None),
            P(("seq", "adapter"), None, None, "tensor"),
            P(None, None, "tensor"),
            P(None, "tensor"),
            P("tensor"),
            P("tensor", None),
            P("adapter", "seq", None),
        ),
        out_specs=P("adapter", "seq", "tensor"),
        check_vma=False,
    )
```
